512 devices in a mesh: segment: 4 (over y_lo, core), ctx: 32 (over z, y_hi), head: 4 (over x).
Axes of the slice: x: 4, y: 4 (y_hi: 2, y_lo: 2; y = y_hi * 2 + y_lo), z: 16, core: 2. Of those that a mesh axis runs over, the one named last changes fastest.
Arguments:
- hidden: bfloat16 [4, 8192, 2880], P('segment', 'ctx', 'head'), may hold values from -450 to 450
- merge_weight: bfloat16 [3, 2880, 2880], P(None, 'head', 'segment'), may hold values from -0.0625 to 0.0625
- query_weight: bfloat16 [5760, 2048], P('ctx', ('segment', 'head')), may hold values from -1 to 1
- key_weight: bfloat16 [5760, 256], P('ctx', 'segment'), may hold values from -8 to 8
- value_weight: bfloat16 [5760, 256], P('ctx', 'segment'), may hold values from -0.078125 to 0.078125
- block_order: int32 [64], replicated, may hold values from 0 to 63, each once
Outputs:
- attended: bfloat16 [8192, 2048], P('ctx', ('segment', 'head'))
The draws below stay inside these ranges and needn't reach their ends.
Inputs may be any that keep to these rules, and one draw needn't show every extreme that they name: `block_order`: a permutation of the sequence blocks.
All inputs are finite; a program needn't handle non-finite values.
Results may differ from the reference program's by a relative error of at most 0.023.
The reference program's roundings to bfloat16 on the way count: a program that leaves them out, or rounds other values in their place, can miss the bound.
Values may be sent and summed in bfloat16 or wider, within the bound.
No kernel may reach another device: no remote copies, remote signals or barrier semaphores. Data moves between devices by JAX's collectives and lax.ppermute only.
A program may use at most 64 MiB of HBM per device.

```python
import math
import jax
import jax.numpy as jnp
from jax import lax

H = 2880
HD = 64
QH = 32
KVH = 4
TOKENS = 8192
BLK = 128
NBLK = 64


def draw_hidden(key, part):
    base_key = jax.random.fold_in(key, 11)
    row_key = jax.random.fold_in(key, 12)
    col_key = jax.random.fold_in(key, 13)
    shape_full = (4, TOKENS, H)
    values_drawn = jax.random.truncated_normal(base_key, -4.0, 4.0, shape_full, jnp.float32)
    top_scale = math.log(10.0)
    row_scale = jnp.exp(jax.random.uniform(row_key, (4, TOKENS, 1), jnp.float32, 0.0, top_scale))
    col_scale = jnp.exp(jax.random.uniform(col_key, (4, 1, H), jnp.float32, 0.0, top_scale))
    return (values_drawn * row_scale * col_scale).astype(jnp.bfloat16)


def query_base(key):
    base_key = jax.random.fold_in(key, 101)
    drawn = jax.random.truncated_normal(base_key, -4.0, 4.0, (2 * H, QH * HD), jnp.float32)
    return drawn / math.sqrt(2.0 * H)


def draw_query_weight(key, part):
    return query_base(key).astype(jnp.bfloat16)


def draw_key_weight(key, part):
    noise_key = jax.random.fold_in(key, 202)
    noise = jax.random.truncated_normal(noise_key, -4.0, 4.0, (2 * H, KVH * HD), jnp.float32) / math.sqrt(2.0 * H)
    return noise.astype(jnp.bfloat16)


def level_of(own_key, extent, cuts, low, largest):
    def one(dim, blocks):
        heights = jax.random.uniform(jax.random.fold_in(jax.random.fold_in(own_key, 6), dim), (blocks,), jnp.float32, low / len(cuts), largest / len(cuts))
        return jnp.repeat(jnp.exp(heights), extent[dim] // blocks).reshape((-1,) + (1,) * (len(extent) - dim - 1))

    gain = one(*cuts[0])
    for cut in cuts[1:]:
        gain = gain * one(*cut)
    return gain


def centred(own_key, extent, width, most, split=(), kind=jnp.bfloat16):
    values = width * jax.random.normal(own_key, extent, jnp.float32)
    if split:
        values = values * level_of(own_key, extent, split, -0.22, 0.18)
    return jnp.clip(values, -most, most).astype(kind)


def setup_inputs(seed: int = 0) -> dict:
    seeds = jax.random.split(jax.random.key(seed), 7)
    return {
        "hidden": draw_hidden(jax.random.fold_in(seeds[6], 71), 0),
        "merge_weight": centred(seeds[1], (3, H, H), (3 * H) ** -0.5, 0.0625, ((1, 4), (2, 4))),
        "query_weight": draw_query_weight(jax.random.fold_in(seeds[6], 71), 0),
        "key_weight": draw_key_weight(jax.random.fold_in(seeds[6], 71), 0),
        "value_weight": centred(seeds[4], (2 * H, KVH * HD), (2 * H) ** -0.5, 0.078125, ((0, 32), (1, 4))),
        "block_order": jax.random.permutation(seeds[5], NBLK).astype(jnp.int32),
    }


def normalize(matrix):
    widened = matrix.astype(jnp.float32)
    return widened * lax.rsqrt(lax.optimization_barrier(jnp.mean(widened * widened, axis=-1, keepdims=True)) + 1e-06)

def reference(hidden, merge_weight, query_weight, key_weight, value_weight, block_order):
    merged_rows = jnp.dot(hidden[0], merge_weight[0], preferred_element_type=jnp.float32)
    merged_rows = merged_rows + jnp.dot(hidden[1], merge_weight[1], preferred_element_type=jnp.float32)
    merged_rows = merged_rows + jnp.dot(hidden[2], merge_weight[2], preferred_element_type=jnp.float32)
    merged_rows = merged_rows.astype(jnp.bfloat16)
    draft_input = jnp.concatenate([normalize(hidden[3]), normalize(merged_rows)], axis=1).astype(jnp.bfloat16)
    queries = jnp.dot(draft_input, query_weight, preferred_element_type=jnp.float32).astype(jnp.bfloat16)
    key_vectors = jnp.dot(draft_input, key_weight, preferred_element_type=jnp.float32).astype(jnp.bfloat16)
    values = jnp.dot(draft_input, value_weight, preferred_element_type=jnp.float32).astype(jnp.bfloat16)
    rows_all = jnp.arange(TOKENS, dtype=jnp.int32)
    positions = block_order[rows_all // BLK] * BLK + rows_all % BLK
    group_size = QH // KVH
    query_block = math.gcd(TOKENS, 1024)

    def head_out(head_id):
        query_head = lax.dynamic_slice_in_dim(queries, head_id * HD, HD, 1)
        pair_index = head_id // group_size
        key_head = lax.dynamic_slice_in_dim(key_vectors, pair_index * HD, HD, 1)
        value_head = lax.dynamic_slice_in_dim(values, pair_index * HD, HD, 1)

        def block_out(block_index):
            row_start = block_index * query_block
            query_rows = lax.dynamic_slice_in_dim(query_head, row_start, query_block, 0)
            query_pos = lax.dynamic_slice_in_dim(positions, row_start, query_block, 0)
            scores = jnp.dot(query_rows, key_head.T, preferred_element_type=jnp.float32) * 0.125
            allowed = positions[None, :] <= query_pos[:, None]
            scores = jnp.where(allowed, scores, -1e+30)
            row_top = lax.optimization_barrier(jnp.max(scores, axis=1, keepdims=True))
            unscaled = jnp.where(allowed, jnp.exp(scores - row_top), 0.0)
            row_total = lax.optimization_barrier(jnp.sum(unscaled, axis=1, keepdims=True))
            mixed_rows = jnp.dot(unscaled.astype(jnp.bfloat16), value_head, preferred_element_type=jnp.float32)
            return (mixed_rows / row_total).astype(jnp.bfloat16)
        blocks_out = lax.map(block_out, jnp.arange(TOKENS // query_block, dtype=jnp.int32))
        return blocks_out.reshape(TOKENS, HD)
    per_head = lax.map(head_out, jnp.arange(QH, dtype=jnp.int32))
    return jnp.transpose(per_head, (1, 0, 2)).reshape(TOKENS, QH * HD)
```

```python
import jax
import jax.numpy as jnp
from jax import lax
from jax.experimental import pallas as pl
from jax.experimental.pallas import tpu as pltpu
from jax.sharding import Mesh, PartitionSpec as P

HD = 64
BLK = 128
SEG = ("yl", "core")
CTX = ("z", "yh")
VMEM = pl.BlockSpec(memory_space=pltpu.VMEM)
DIM0 = (((0,), (0,)), ((), ()))


def project_kernel(rows_ref, weights_ref, quarter_ref, query_ref, kv_ref, sent_ref):
    n_x, n_seg, _, chunk, tokens = rows_ref.shape
    width = n_x * n_seg * chunk
    scales = []
    for kind in range(2):
        total = jnp.zeros((1, tokens), jnp.float32)
        for i in range(n_x):
            for s in range(n_seg):
                part = rows_ref[i, s, kind].astype(jnp.float32)
                total = total + jnp.sum(part * part, axis=0, keepdims=True)
        scales.append(lax.rsqrt(total / width + 1e-06))
    acc = jnp.zeros((weights_ref.shape[2], tokens), jnp.float32)
    for kind in range(2):
        for i in range(n_x):
            for s in range(n_seg):
                at = i * n_seg + s if kind == 0 else n_x * n_seg + s * n_x + i
                normed = (rows_ref[i, s, kind].astype(jnp.float32) * scales[kind]).astype(jnp.bfloat16)
                acc = acc + lax.dot_general(weights_ref[at], normed, DIM0, preferred_element_type=jnp.float32)
    half = acc.shape[0] // 2
    query_ref[...] = acc[:half].astype(jnp.bfloat16)
    kv_ref[...] = acc[half:].T.astype(jnp.bfloat16)
    size = sent_ref.shape[1]
    start = pl.multiple_of(quarter_ref[0] * size, size)
    quarter = kv_ref[pl.ds(start, size), :]
    for i in range(sent_ref.shape[0]):
        sent_ref[i] = quarter


def attend_kernel(query_ref, own_ref, all_ref, bias_ref, out_ref):
    zeros = jnp.zeros((HD, BLK), jnp.bfloat16)
    pieces = []
    for a in range(2):
        for g in range(2):
            piece = query_ref[g * HD : (g + 1) * HD, a * BLK : (a + 1) * BLK] * jnp.bfloat16(0.125)
            pieces.append(jnp.concatenate([piece, zeros], axis=0))
    queries = jnp.concatenate(pieces, axis=1)
    lanes = queries.shape[1]
    key_row = lax.broadcasted_iota(jnp.int32, (BLK, lanes // 2), 0)
    query_row = lax.broadcasted_iota(jnp.int32, (BLK, lanes // 2), 1) % BLK
    tops, totals, accums = [], [], []
    for a in range(2):
        own = own_ref[a * BLK : (a + 1) * BLK, :]
        scores = jnp.dot(own, queries[:, a * 2 * BLK : (a + 1) * 2 * BLK], preferred_element_type=jnp.float32)
        scores = jnp.where(key_row <= query_row, scores, -1e30)
        top = jnp.max(scores, axis=0, keepdims=True)
        weights = jnp.exp(scores - top)
        tops.append(top)
        totals.append(jnp.sum(weights, axis=0, keepdims=True))
        accums.append(lax.dot_general(own, weights.astype(jnp.bfloat16), DIM0, preferred_element_type=jnp.float32))
    top, total, accum = (jnp.concatenate(v, axis=1) for v in (tops, totals, accums))
    groups, chunk, _ = all_ref.shape
    step = 16

    def one(turn, carry):
        top, total, accum = carry
        first = pl.multiple_of(turn * step, step)
        keys = all_ref[pl.ds(first, step)].reshape(step * chunk, 2 * HD)
        bias = bias_ref[pl.ds(first, step), :]
        scores = jnp.dot(keys, queries, preferred_element_type=jnp.float32)
        scores = scores.reshape(step, chunk, lanes)
        highest = jnp.max(scores, axis=1) + bias
        new_top = jnp.maximum(top, jnp.max(highest, axis=0, keepdims=True))
        weights = jnp.exp(scores + (bias - new_top)[:, None, :])
        rescale = jnp.exp(top - new_top)
        total = total * rescale + jnp.sum(weights.reshape(step * chunk, lanes), axis=0, keepdims=True)
        mixed = lax.dot_general(
            keys,
            weights.reshape(step * chunk, lanes).astype(jnp.bfloat16),
            DIM0,
            preferred_element_type=jnp.float32,
        )
        return new_top, total, accum * rescale + mixed

    top, total, accum = lax.fori_loop(0, groups // step, one, (top, total, accum))
    result = accum[HD:] / total
    for a in range(2):
        left = result[:, 2 * a * BLK : (2 * a + 1) * BLK]
        right = result[:, (2 * a + 1) * BLK : (2 * a + 2) * BLK]
        out_ref[a * BLK : (a + 1) * BLK, :] = jnp.concatenate([left, right], axis=0).T.astype(jnp.bfloat16)


def body(hidden, merge_weight, query_weight, key_weight, value_weight, block_order):
    tokens, features = hidden.shape[1:]
    n_x, n_seg = lax.axis_size("x"), lax.axis_size(SEG)
    n_ctx = lax.axis_size(CTX)
    x_id, seg_id, ctx_id = lax.axis_index("x"), lax.axis_index(SEG), lax.axis_index(CTX)
    chunk = features // n_seg

    weights = jnp.concatenate([query_weight, key_weight, value_weight], axis=1)
    weights = lax.all_gather(weights, "yh", axis=0)
    weights = lax.all_gather(weights, "z", axis=0)
    weights = weights.reshape(n_ctx, *weights.shape[2:])

    turned = hidden[0].T
    half = features // 2
    low = lax.all_gather(turned[:half], SEG, axis=0)
    high = lax.all_gather(turned[half:], SEG, axis=0)
    sections = jnp.concatenate([low, high], axis=1)
    partial = jnp.einsum("kft,kfc->ct", sections[:3], merge_weight, preferred_element_type=jnp.float32)
    parts = lax.all_to_all(partial.reshape(n_x, chunk, tokens), "x", 0, 0)
    merged = jnp.sum(parts, axis=0).astype(jnp.bfloat16)
    embed = lax.dynamic_slice_in_dim(sections[3], seg_id * chunk, chunk, 0)
    rows = jnp.stack([embed, merged])
    rows = lax.all_gather(rows, SEG, axis=0)
    rows = lax.all_to_all(jnp.broadcast_to(rows, (n_x, *rows.shape)), "x", 0, 0)

    quarter = tokens // n_x
    query, own_kv, sent = pl.pallas_call(
        project_kernel,
        out_shape=(
            jax.ShapeDtypeStruct((2 * HD, tokens), jnp.bfloat16),
            jax.ShapeDtypeStruct((tokens, 2 * HD), jnp.bfloat16),
            jax.ShapeDtypeStruct((n_ctx, quarter, 2 * HD), jnp.bfloat16),
        ),
        in_specs=[VMEM, VMEM, pl.BlockSpec(memory_space=pltpu.SMEM)],
        out_specs=(VMEM, VMEM, VMEM),
        compiler_params=pltpu.CompilerParams(vmem_limit_bytes=40 << 20),
        name="project",
    )(rows, weights, x_id.reshape(1))

    taken = lax.all_to_all(sent, ("yh", "z"), 0, 0)
    taken = lax.all_to_all(jnp.broadcast_to(taken, (n_x, *taken.shape)), "x", 0, 0)
    taken = taken.reshape(n_x * n_ctx, quarter, 2 * HD)

    n_z, n_yh = lax.axis_size("z"), lax.axis_size("yh")
    placed = block_order.reshape(n_z, n_yh, 2).transpose(2, 1, 0)
    placed = jnp.repeat(placed, n_x // 2, axis=0).reshape(n_x * n_ctx)
    mine = lax.dynamic_slice_in_dim(block_order, ctx_id * 2, 2, 0)
    mine = jnp.repeat(mine, 2 * BLK)
    bias = jnp.where(placed[:, None] < mine[None, :], 0.0, -1e30).astype(jnp.float32)

    return pl.pallas_call(
        attend_kernel,
        out_shape=jax.ShapeDtypeStruct((tokens, 2 * HD), jnp.bfloat16),
        in_specs=[VMEM, VMEM, VMEM, VMEM],
        out_specs=VMEM,
        compiler_params=pltpu.CompilerParams(vmem_limit_bytes=40 << 20),
        name="attend",
    )(query, own_kv, taken, bias)


def solution(mesh):
    shape = mesh.shape
    grid = mesh.devices.reshape(2, shape["segment"] // 2, shape["ctx"] // 2, 2, shape["head"])
    fine = Mesh(grid, ("yl", "core", "z", "yh", "x"))
    return jax.shard_map(
        body,
        mesh=fine,
        in_specs=(
            P(SEG, CTX, "x"),
            P(None, "x", SEG),
            P(CTX, (*SEG, "x")),
            P(CTX, SEG),
            P(CTX, SEG),
            P(),
        ),
        out_specs=P(CTX, (*SEG, "x")),
        check_vma=False,
    )
```

```python
import jax
import jax.numpy as jnp
from jax import lax
from jax.experimental import pallas as pl
from jax.experimental.pallas import tpu as pltpu
from jax.sharding import Mesh, PartitionSpec as P

HD = 64
BLK = 128
SEG = ("yl", "core")
CTX = ("z", "yh")
VMEM = pl.BlockSpec(memory_space=pltpu.VMEM)
DIM0 = (((0,), (0,)), ((), ()))


def pack_kernel(query_ref, key_ref, value_ref, out_ref):
    turned = jnp.concatenate([key_ref[...], value_ref[...]], axis=0).astype(jnp.float32)
    out_ref[:, : query_ref.shape[1]] = query_ref[...]
    out_ref[:, query_ref.shape[1] :] = turned.T.astype(jnp.bfloat16)


def merge_kernel(low_ref, high_ref, weight_ref, place_ref, partial_ref, embed_ref, hold_ref):
    split, total = low_ref.shape[1], weight_ref.shape[1]
    chunks, chunk, _ = partial_ref.shape
    hold_ref[:split] = low_ref[3].astype(jnp.float32)
    hold_ref[split:] = high_ref[3].astype(jnp.float32)
    embed_ref[...] = jnp.zeros_like(embed_ref)
    for half in range(2):
        first, second = hold_ref[pl.ds(half * chunk, chunk), :], hold_ref[pl.ds((2 + half) * chunk, chunk), :]
        block = jnp.where(place_ref[0] == 0, first, second).astype(jnp.bfloat16)
        for i in range(chunks):
            embed_ref[2 * i + half, :chunk] = block
    acc = None
    for k in range(3):
        for ref, rows in ((low_ref, slice(0, split)), (high_ref, slice(split, total))):
            term = lax.dot_general(weight_ref[k, rows, :], ref[k], DIM0, preferred_element_type=jnp.float32)
            acc = term if acc is None else acc + term
    hold_ref[...] = acc
    for i in range(chunks):
        partial_ref[i] = hold_ref[pl.ds(i * chunk, chunk), :]


def settle_kernel(parts_ref, out_ref):
    total = parts_ref[0]
    for i in range(1, parts_ref.shape[0]):
        total = total + parts_ref[i]
    out_ref[...] = jnp.zeros_like(out_ref)
    out_ref[: parts_ref.shape[1]] = total.astype(jnp.bfloat16)


def spread_kernel(block_ref, out_ref):
    count = block_ref.shape[0]
    for i in range(out_ref.shape[0] // count):
        out_ref[i * count : (i + 1) * count] = block_ref[...]


def project_kernel(
    embed_own, embed_other, merged_own, merged_other, weights_ref, place_ref, query_ref, sent_ref
):
    core, x_id = place_ref[0], place_ref[1]
    chunks, _, tokens = embed_own.shape
    chunk = weights_ref.shape[1]
    width = 2 * chunks * chunk
    acc = jnp.zeros((weights_ref.shape[2], tokens), jnp.float32)
    for kind, pair in enumerate(((embed_own, embed_other), (merged_own, merged_other))):
        total = jnp.zeros((1, tokens), jnp.float32)
        for ref in pair:
            for i in range(chunks):
                part = ref[i, :chunk].astype(jnp.float32)
                total = total + jnp.sum(part * part, axis=0, keepdims=True)
        scale = lax.rsqrt(total / width + 1e-06)
        for ref, side in zip(pair, (core, 1 - core)):
            for i in range(chunks):
                if kind == 0:
                    at = i // 2 * 4 + 2 * side + i % 2
                else:
                    at = 2 * chunks + (2 * (i % 2) + side) * 4 + i // 2
                normed = (ref[i, :chunk].astype(jnp.float32) * scale).astype(jnp.bfloat16)
                acc = acc + lax.dot_general(weights_ref[at], normed, DIM0, preferred_element_type=jnp.float32)
    half = acc.shape[0] // 2
    query_ref[...] = acc[:half].astype(jnp.bfloat16)
    rows = acc[half:].T.astype(jnp.bfloat16)
    size = sent_ref.shape[1]
    quarter = rows[:size]
    for i in range(1, tokens // size):
        quarter = jnp.where(x_id == i, rows[i * size : (i + 1) * size], quarter)
    for i in range(sent_ref.shape[0]):
        sent_ref[i] = quarter


def attend_kernel(query_ref, sent_ref, all_ref, bias_ref, place_ref, out_ref):
    x_id = place_ref[1]
    own = sent_ref[0]
    groups, chunk, _ = all_ref.shape
    zeros = jnp.zeros((HD, BLK), jnp.bfloat16)
    lanes = 4 * BLK
    key_row = lax.broadcasted_iota(jnp.int32, (chunk, lanes), 0) + (x_id % 2) * chunk
    lane = lax.broadcasted_iota(jnp.int32, (chunk, lanes), 1)
    own_bias = jnp.where((lane // (2 * BLK) == x_id // 2) & (key_row <= lane % BLK), 0.0, -1e30)
    step = 16
    for source in range(query_ref.shape[0]):
        pieces = []
        for a in range(2):
            for g in range(2):
                piece = query_ref[source, g * HD : (g + 1) * HD, a * BLK : (a + 1) * BLK]
                pieces.append(jnp.concatenate([piece * jnp.bfloat16(0.125), zeros], axis=0))
        queries = jnp.concatenate(pieces, axis=1)
        scores = jnp.dot(own, queries, preferred_element_type=jnp.float32) + own_bias
        top = jnp.maximum(jnp.max(scores, axis=0, keepdims=True), -1e20)
        weights = jnp.exp(scores - top)
        total = jnp.sum(weights, axis=0, keepdims=True)
        accum = lax.dot_general(own, weights.astype(jnp.bfloat16), DIM0, preferred_element_type=jnp.float32)
        for first in range(0, groups, step):
            keys = all_ref[first : first + step].reshape(step * chunk, 2 * HD)
            bias = bias_ref[first : first + step, :]
            scores = jnp.dot(keys, queries, preferred_element_type=jnp.float32)
            scores = scores.reshape(step, chunk, lanes)
            highest = jnp.max(scores, axis=1) + bias
            new_top = jnp.maximum(top, jnp.max(highest, axis=0, keepdims=True))
            weights = jnp.exp(scores + (bias - new_top)[:, None, :])
            rescale = jnp.exp(top - new_top)
            weights = weights.reshape(step * chunk, lanes)
            total = total * rescale + jnp.sum(weights, axis=0, keepdims=True)
            mixed = lax.dot_general(
                keys, weights.astype(jnp.bfloat16), DIM0, preferred_element_type=jnp.float32
            )
            accum = accum * rescale + mixed
            top = new_top
        out_ref[source, :HD] = accum[HD:]
        row = lax.broadcasted_iota(jnp.int32, (8, lanes), 0)
        out_ref[source, HD:] = jnp.where(row == 0, top, total)


def combine_kernel(parts_ref, out_ref):
    count = parts_ref.shape[0]
    tops = [parts_ref[i, HD : HD + 1, :] for i in range(count)]
    top = tops[0]
    for i in range(1, count):
        top = jnp.maximum(top, tops[i])
    total = jnp.zeros_like(top)
    accum = jnp.zeros((HD, parts_ref.shape[2]), jnp.float32)
    for i in range(count):
        share = jnp.exp(tops[i] - top)
        total = total + parts_ref[i, HD + 1 : HD + 2, :] * share
        accum = accum + parts_ref[i, :HD, :] * share
    result = accum / total
    for a in range(2):
        left = result[:, 2 * a * BLK : (2 * a + 1) * BLK]
        right = result[:, (2 * a + 1) * BLK : (2 * a + 2) * BLK]
        out_ref[a * BLK : (a + 1) * BLK, :] = jnp.concatenate([left, right], axis=0).T.astype(jnp.bfloat16)


def body(hidden, merge_weight, query_weight, key_weight, value_weight, block_order):
    tokens, features = hidden.shape[1:]
    n_x, n_seg = lax.axis_size("x"), lax.axis_size(SEG)
    n_ctx = lax.axis_size(CTX)
    x_id, core, ctx_id = lax.axis_index("x"), lax.axis_index("core"), lax.axis_index(CTX)
    chunk = features // n_seg
    smem = pl.BlockSpec(memory_space=pltpu.SMEM)
    place = jnp.stack([core, x_id]).astype(jnp.int32)

    packed = pl.pallas_call(
        pack_kernel,
        out_shape=jax.ShapeDtypeStruct((query_weight.shape[0], 4 * HD), jnp.bfloat16),
        in_specs=[VMEM] * 3,
        out_specs=VMEM,
        name="pack",
    )(query_weight, key_weight.T, value_weight.T)
    weights = lax.all_gather(packed, "yh", axis=0)
    weights = lax.all_gather(weights, "z", axis=0)
    weights = weights.reshape(n_ctx, *weights.shape[2:])

    turned = hidden[0].T
    split = (features // 2 + 15) // 16 * 16
    low = lax.all_gather(turned[:split], SEG, axis=0)
    high = lax.all_gather(turned[split:], SEG, axis=0)

    padded = (chunk + 7) // 8 * 8
    partial, embed = pl.pallas_call(
        merge_kernel,
        out_shape=(
            jax.ShapeDtypeStruct((n_x, chunk, tokens), jnp.float32),
            jax.ShapeDtypeStruct((2 * n_x, padded, tokens), jnp.bfloat16),
        ),
        in_specs=[VMEM] * 3 + [smem],
        out_specs=(VMEM, VMEM),
        scratch_shapes=[pltpu.VMEM((features, tokens), jnp.float32)],
        compiler_params=pltpu.CompilerParams(vmem_limit_bytes=40 << 20),
        name="merge",
    )(low, high, merge_weight, place)
    parts = lax.all_to_all(partial, "x", 0, 0)
    merged = pl.pallas_call(
        settle_kernel,
        out_shape=jax.ShapeDtypeStruct((padded, tokens), jnp.bfloat16),
        in_specs=[VMEM],
        out_specs=VMEM,
        name="settle",
    )(parts)
    merged = lax.all_gather(merged, "yl", axis=0)
    merged = pl.pallas_call(
        spread_kernel,
        out_shape=jax.ShapeDtypeStruct((2 * n_x, padded, tokens), jnp.bfloat16),
        in_specs=[VMEM],
        out_specs=VMEM,
        name="spread",
    )(merged)

    def over_x(copies):
        own = lax.all_to_all(copies, "x", 0, 0, tiled=True)
        return own, lax.ppermute(own, "core", [(0, 1), (1, 0)])

    embed_own, embed_other = over_x(embed)
    merged_own, merged_other = over_x(merged)

    quarter = tokens // n_x
    query, sent = pl.pallas_call(
        project_kernel,
        out_shape=(
            jax.ShapeDtypeStruct((2 * HD, tokens), jnp.bfloat16),
            jax.ShapeDtypeStruct((n_ctx, quarter, 2 * HD), jnp.bfloat16),
        ),
        in_specs=[VMEM] * 5 + [smem],
        out_specs=(VMEM, VMEM),
        compiler_params=pltpu.CompilerParams(vmem_limit_bytes=40 << 20),
        name="project",
    )(embed_own, embed_other, merged_own, merged_other, weights, place)

    queries = lax.all_gather(query, "x", axis=0)
    taken = lax.all_to_all(sent, ("yh", "z"), 0, 0)

    n_z, n_yh = lax.axis_size("z"), lax.axis_size("yh")
    placed = block_order.reshape(n_z, n_yh, 2).transpose(2, 1, 0).reshape(2, n_ctx)
    placed = jnp.where(x_id < n_x // 2, placed[0], placed[1])
    mine = lax.dynamic_slice_in_dim(block_order, ctx_id * 2, 2, 0)
    bias = jnp.where(placed[:, None] < jnp.repeat(mine, 2 * BLK)[None, :], 0.0, -1e30).astype(jnp.float32)

    parts = pl.pallas_call(
        attend_kernel,
        out_shape=jax.ShapeDtypeStruct((n_x, HD + 8, 4 * BLK), jnp.float32),
        in_specs=[VMEM] * 4 + [smem],
        out_specs=VMEM,
        compiler_params=pltpu.CompilerParams(vmem_limit_bytes=40 << 20),
        name="attend",
    )(queries, sent, taken, bias, place)
    parts = lax.all_to_all(parts, "x", 0, 0)
    return pl.pallas_call(
        combine_kernel,
        out_shape=jax.ShapeDtypeStruct((tokens, 2 * HD), jnp.bfloat16),
        in_specs=[VMEM],
        out_specs=VMEM,
        name="combine",
    )(parts)


def solution(mesh):
    shape = mesh.shape
    grid = mesh.devices.reshape(2, shape["segment"] // 2, shape["ctx"] // 2, 2, shape["head"])
    fine = Mesh(grid, ("yl", "core", "z", "yh", "x"))
    return jax.shard_map(
        body,
        mesh=fine,
        in_specs=(
            P(SEG, CTX, "x"),
            P(None, "x", SEG),
            P(CTX, (*SEG, "x")),
            P(CTX, SEG),
            P(CTX, SEG),
            P(),
        ),
        out_specs=P(CTX, (*SEG, "x")),
        check_vma=False,
    )
```

```python
import jax
import jax.numpy as jnp
from jax import lax
from jax.experimental import pallas as pl
from jax.experimental.pallas import tpu as pltpu
from jax.sharding import Mesh, PartitionSpec as P

HD = 64
BLK = 128
SEG = ("yl", "core")
CTX = ("z", "yh")
VMEM = pl.BlockSpec(memory_space=pltpu.VMEM)
DIM0 = (((0,), (0,)), ((), ()))


def pack_kernel(query_ref, key_ref, value_ref, out_ref):
    turned = jnp.concatenate([key_ref[...], value_ref[...]], axis=0).astype(jnp.float32)
    out_ref[:, : query_ref.shape[1]] = query_ref[...]
    out_ref[:, query_ref.shape[1] :] = turned.T.astype(jnp.bfloat16)


def merge_kernel(low_ref, high_ref, weight_ref, place_ref, partial_ref, embed_ref, hold_ref):
    split, total = low_ref.shape[1], weight_ref.shape[1]
    chunks, chunk, _ = partial_ref.shape
    hold_ref[:split] = low_ref[3].astype(jnp.float32)
    hold_ref[split:] = high_ref[3].astype(jnp.float32)
    embed_ref[...] = jnp.zeros_like(embed_ref)
    for half in range(2):
        first, second = hold_ref[pl.ds(half * chunk, chunk), :], hold_ref[pl.ds((2 + half) * chunk, chunk), :]
        block = jnp.where(place_ref[0] == 0, first, second).astype(jnp.bfloat16)
        for i in range(chunks):
            embed_ref[2 * i + half, :chunk] = block
    acc = None
    for k in range(3):
        for ref, rows in ((low_ref, slice(0, split)), (high_ref, slice(split, total))):
            term = lax.dot_general(weight_ref[k, rows, :], ref[k], DIM0, preferred_element_type=jnp.float32)
            acc = term if acc is None else acc + term
    hold_ref[...] = acc
    for i in range(chunks):
        partial_ref[i] = hold_ref[pl.ds(i * chunk, chunk), :]


def settle_kernel(parts_ref, out_ref):
    total = parts_ref[0]
    for i in range(1, parts_ref.shape[0]):
        total = total + parts_ref[i]
    out_ref[...] = jnp.zeros_like(out_ref)
    out_ref[: parts_ref.shape[1]] = total.astype(jnp.bfloat16)


def spread_kernel(block_ref, out_ref):
    count = block_ref.shape[0]
    for i in range(out_ref.shape[0] // count):
        out_ref[i * count : (i + 1) * count] = block_ref[...]


def norm_kernel(embed_own, embed_other, merged_own, merged_other, place_ref, out_ref):
    core = place_ref[0]
    chunks = embed_own.shape[0]
    chunk = out_ref.shape[1]
    width = 2 * chunks * chunk
    for kind, pair in enumerate(((embed_own, embed_other), (merged_own, merged_other))):
        total = jnp.zeros((1, out_ref.shape[2]), jnp.float32)
        for ref in pair:
            for i in range(chunks):
                part = ref[i, :chunk].astype(jnp.float32)
                total = total + jnp.sum(part * part, axis=0, keepdims=True)
        scale = lax.rsqrt(total / width + 1e-06)
        for ref, side in zip(pair, (core, 1 - core)):
            for i in range(chunks):
                if kind == 0:
                    at = i // 2 * 4 + 2 * side + i % 2
                else:
                    at = 2 * chunks + (2 * (i % 2) + side) * 4 + i // 2
                out_ref[at] = (ref[i, :chunk].astype(jnp.float32) * scale).astype(jnp.bfloat16)


def project_kernel(
    rows_hbm, weights_hbm, place_ref, query_ref, sent_ref, own_ref, rows_ref, weights_ref, arrived
):
    x_id = place_ref[1]
    pieces = arrived.shape[1]
    count = weights_ref.shape[0] // pieces
    copies = []
    for p in range(pieces):
        span = pl.ds(p * count, count)
        both = ((rows_hbm, rows_ref), (weights_hbm, weights_ref))
        copies.append(
            [pltpu.make_async_copy(src.at[span], dst.at[span], arrived.at[k, p]) for k, (src, dst) in enumerate(both)]
        )
        for copy in copies[-1]:
            copy.start()
    tokens = rows_ref.shape[2]
    acc = jnp.zeros((weights_ref.shape[2], tokens), jnp.float32)
    for p in range(pieces):
        for copy in copies[p]:
            copy.wait()
        for at in range(p * count, (p + 1) * count):
            acc = acc + lax.dot_general(weights_ref[at], rows_ref[at], DIM0, preferred_element_type=jnp.float32)
    half = acc.shape[0] // 2
    query_ref[...] = acc[:half].astype(jnp.bfloat16)
    rows = acc[half:].T.astype(jnp.bfloat16)
    size = sent_ref.shape[1]
    quarter = rows[:size]
    for i in range(1, tokens // size):
        quarter = jnp.where(x_id == i, rows[i * size : (i + 1) * size], quarter)
    for i in range(sent_ref.shape[0]):
        sent_ref[i] = quarter
    own_ref[...] = quarter


def heads_of(query_ref, source):
    zeros = jnp.zeros((HD, BLK), jnp.bfloat16)
    pieces = []
    for a in range(2):
        for g in range(2):
            piece = query_ref[source, g * HD : (g + 1) * HD, a * BLK : (a + 1) * BLK]
            pieces.append(jnp.concatenate([piece * jnp.bfloat16(0.125), zeros], axis=0))
    return jnp.concatenate(pieces, axis=1)


def attend_keys(queries, keys_ref, bias_ref, state):
    top, total, accum = state
    groups, chunk, _ = keys_ref.shape
    keys = keys_ref[...].reshape(groups * chunk, 2 * HD)
    bias = bias_ref[...]
    scores = jnp.dot(keys, queries, preferred_element_type=jnp.float32)
    scores = scores.reshape(groups, chunk, queries.shape[1])
    highest = jnp.max(scores, axis=1) + bias
    new_top = jnp.maximum(top, jnp.max(highest, axis=0, keepdims=True))
    weights = jnp.exp(scores + (bias - new_top)[:, None, :])
    rescale = jnp.exp(top - new_top)
    weights = weights.reshape(groups * chunk, queries.shape[1])
    total = total * rescale + jnp.sum(weights, axis=0, keepdims=True)
    mixed = lax.dot_general(keys, weights.astype(jnp.bfloat16), DIM0, preferred_element_type=jnp.float32)
    return new_top, total, accum * rescale + mixed[HD:]


def store_state(out_ref, source, state):
    top, total, accum = state
    out_ref[source, :HD] = accum
    row = lax.broadcasted_iota(jnp.int32, (8, accum.shape[1]), 0)
    out_ref[source, HD:] = jnp.where(row == 0, top, total)


def first_kernel(query_ref, own_ref, keys_ref, bias_ref, place_ref, out_ref):
    x_id = place_ref[1]
    own = own_ref[...]
    chunk = own.shape[0]
    lanes = out_ref.shape[2]
    key_row = lax.broadcasted_iota(jnp.int32, (chunk, lanes), 0) + (x_id % 2) * chunk
    lane = lax.broadcasted_iota(jnp.int32, (chunk, lanes), 1)
    own_bias = jnp.where((lane // (2 * BLK) == x_id // 2) & (key_row <= lane % BLK), 0.0, -1e30)
    for source in range(query_ref.shape[0]):
        queries = heads_of(query_ref, source)
        scores = jnp.dot(own, queries, preferred_element_type=jnp.float32) + own_bias
        top = jnp.maximum(jnp.max(scores, axis=0, keepdims=True), -1e20)
        weights = jnp.exp(scores - top)
        total = jnp.sum(weights, axis=0, keepdims=True)
        accum = lax.dot_general(own, weights.astype(jnp.bfloat16), DIM0, preferred_element_type=jnp.float32)
        store_state(out_ref, source, attend_keys(queries, keys_ref, bias_ref, (top, total, accum[HD:])))


def second_kernel(query_ref, keys_ref, bias_ref, state_ref, out_ref):
    for source in range(query_ref.shape[0]):
        state = (
            state_ref[source, HD : HD + 1, :],
            state_ref[source, HD + 1 : HD + 2, :],
            state_ref[source, :HD, :],
        )
        store_state(out_ref, source, attend_keys(heads_of(query_ref, source), keys_ref, bias_ref, state))


def combine_kernel(parts_ref, out_ref):
    count = parts_ref.shape[0]
    tops = [parts_ref[i, HD : HD + 1, :] for i in range(count)]
    top = tops[0]
    for i in range(1, count):
        top = jnp.maximum(top, tops[i])
    total = jnp.zeros_like(top)
    accum = jnp.zeros((HD, parts_ref.shape[2]), jnp.float32)
    for i in range(count):
        share = jnp.exp(tops[i] - top)
        total = total + parts_ref[i, HD + 1 : HD + 2, :] * share
        accum = accum + parts_ref[i, :HD, :] * share
    result = accum / total
    for a in range(2):
        left = result[:, 2 * a * BLK : (2 * a + 1) * BLK]
        right = result[:, (2 * a + 1) * BLK : (2 * a + 2) * BLK]
        out_ref[a * BLK : (a + 1) * BLK, :] = jnp.concatenate([left, right], axis=0).T.astype(jnp.bfloat16)


def body(hidden, merge_weight, query_weight, key_weight, value_weight, block_order):
    tokens, features = hidden.shape[1:]
    n_x, n_seg = lax.axis_size("x"), lax.axis_size(SEG)
    n_ctx = lax.axis_size(CTX)
    x_id, core, ctx_id = lax.axis_index("x"), lax.axis_index("core"), lax.axis_index(CTX)
    chunk = features // n_seg
    smem, hbm = pl.BlockSpec(memory_space=pltpu.SMEM), pl.BlockSpec(memory_space=pltpu.HBM)
    place = jnp.stack([core, x_id]).astype(jnp.int32)

    packed = pl.pallas_call(
        pack_kernel,
        out_shape=jax.ShapeDtypeStruct((query_weight.shape[0], 4 * HD), jnp.bfloat16),
        in_specs=[VMEM] * 3,
        out_specs=VMEM,
        name="pack",
    )(query_weight, key_weight.T, value_weight.T)
    weights = lax.all_gather(packed, "yh", axis=0)
    weights = lax.all_gather(weights, "z", axis=0)
    weights = weights.reshape(n_ctx, *weights.shape[2:])

    turned = hidden[0].T
    split = (features // 2 + 15) // 16 * 16
    low = lax.all_gather(turned[:split], SEG, axis=0)
    high = lax.all_gather(turned[split:], SEG, axis=0)

    padded = (chunk + 7) // 8 * 8
    partial, embed = pl.pallas_call(
        merge_kernel,
        out_shape=(
            jax.ShapeDtypeStruct((n_x, chunk, tokens), jnp.float32),
            jax.ShapeDtypeStruct((2 * n_x, padded, tokens), jnp.bfloat16),
        ),
        in_specs=[VMEM] * 3 + [smem],
        out_specs=(VMEM, VMEM),
        scratch_shapes=[pltpu.VMEM((features, tokens), jnp.float32)],
        compiler_params=pltpu.CompilerParams(vmem_limit_bytes=40 << 20),
        name="merge",
    )(low, high, merge_weight, place)
    parts = lax.all_to_all(partial, "x", 0, 0)
    merged = pl.pallas_call(
        settle_kernel,
        out_shape=jax.ShapeDtypeStruct((padded, tokens), jnp.bfloat16),
        in_specs=[VMEM],
        out_specs=VMEM,
        name="settle",
    )(parts)
    merged = lax.all_gather(merged, "yl", axis=0)
    merged = pl.pallas_call(
        spread_kernel,
        out_shape=jax.ShapeDtypeStruct((2 * n_x, padded, tokens), jnp.bfloat16),
        in_specs=[VMEM],
        out_specs=VMEM,
        name="spread",
    )(merged)

    def over_x(copies):
        own = lax.all_to_all(copies, "x", 0, 0, tiled=True)
        return own, lax.ppermute(own, "core", [(0, 1), (1, 0)])

    embed_own, embed_other = over_x(embed)
    merged_own, merged_other = over_x(merged)

    quarter = tokens // n_x
    params = pltpu.CompilerParams(vmem_limit_bytes=40 << 20)
    rows = pl.pallas_call(
        norm_kernel,
        out_shape=jax.ShapeDtypeStruct((n_ctx, chunk, tokens), jnp.bfloat16),
        in_specs=[VMEM] * 4 + [smem],
        out_specs=VMEM,
        compiler_params=params,
        name="norm",
    )(embed_own, embed_other, merged_own, merged_other, place)
    n_z, n_yh = lax.axis_size("z"), lax.axis_size("yh")
    query, sent, own = pl.pallas_call(
        project_kernel,
        out_shape=(
            jax.ShapeDtypeStruct((2 * HD, tokens), jnp.bfloat16),
            jax.ShapeDtypeStruct((n_z, quarter, 2 * HD), jnp.bfloat16),
            jax.ShapeDtypeStruct((quarter, 2 * HD), jnp.bfloat16),
        ),
        in_specs=[hbm, hbm, smem],
        out_specs=(VMEM, VMEM, VMEM),
        scratch_shapes=[
            pltpu.VMEM(rows.shape, rows.dtype),
            pltpu.VMEM(weights.shape, weights.dtype),
            pltpu.SemaphoreType.DMA((2, 4)),
        ],
        compiler_params=pltpu.CompilerParams(vmem_limit_bytes=60 << 20),
        name="project",
    )(rows, weights, place)

    taken = lax.all_to_all(sent, "z", 0, 0)
    queries = lax.all_gather(query, "x", axis=0)
    other = lax.ppermute(taken, "yh", [(0, 1), (1, 0)])

    placed = block_order.reshape(n_z, n_yh, 2)
    placed = jnp.where(x_id < n_x // 2, placed[:, :, 0], placed[:, :, 1])
    mine = jnp.repeat(lax.dynamic_slice_in_dim(block_order, ctx_id * 2, 2, 0), 2 * BLK)
    yh = lax.axis_index("yh")
    near = jnp.where(yh == 0, placed[:, 0], placed[:, 1])
    far = jnp.where(yh == 0, placed[:, 1], placed[:, 0])
    near = jnp.where(near[:, None] < mine[None, :], 0.0, -1e30).astype(jnp.float32)
    far = jnp.where(far[:, None] < mine[None, :], 0.0, -1e30).astype(jnp.float32)

    scores = 8 * BLK * 2 * n_z * quarter
    state = jax.ShapeDtypeStruct((n_x, HD + 8, 4 * BLK), jnp.float32)
    cost = pl.CostEstimate(flops=scores * 4 * HD, bytes_accessed=2 << 20, transcendentals=scores)
    parts = pl.pallas_call(
        first_kernel,
        out_shape=state,
        in_specs=[VMEM] * 4 + [smem],
        out_specs=VMEM,
        compiler_params=params,
        cost_estimate=cost,
        name="attend_first",
    )(queries, own, taken, near, place)
    parts = pl.pallas_call(
        second_kernel,
        out_shape=state,
        in_specs=[VMEM] * 4,
        out_specs=VMEM,
        compiler_params=params,
        cost_estimate=cost,
        name="attend_second",
    )(queries, other, far, parts)
    parts = lax.all_to_all(parts, "x", 0, 0)
    return pl.pallas_call(
        combine_kernel,
        out_shape=jax.ShapeDtypeStruct((tokens, 2 * HD), jnp.bfloat16),
        in_specs=[VMEM],
        out_specs=VMEM,
        name="combine",
    )(parts)


def solution(mesh):
    shape = mesh.shape
    grid = mesh.devices.reshape(2, shape["segment"] // 2, shape["ctx"] // 2, 2, shape["head"])
    fine = Mesh(grid, ("yl", "core", "z", "yh", "x"))
    return jax.shard_map(
        body,
        mesh=fine,
        in_specs=(
            P(SEG, CTX, "x"),
            P(None, "x", SEG),
            P(CTX, (*SEG, "x")),
            P(CTX, SEG),
            P(CTX, SEG),
            P(),
        ),
        out_specs=P(CTX, (*SEG, "x")),
        check_vma=False,
    )
```

```python
import jax
import jax.numpy as jnp
from jax import lax
from jax.experimental import pallas as pl
from jax.experimental.pallas import tpu as pltpu
from jax.sharding import Mesh, PartitionSpec as P

HD = 64
BLK = 128
SEG = ("yl", "core")
CTX = ("z", "yh")
VMEM = pl.BlockSpec(memory_space=pltpu.VMEM)
DIM0 = (((0,), (0,)), ((), ()))


def pack_kernel(query_ref, key_ref, value_ref, out_ref):
    turned = jnp.concatenate([key_ref[...], value_ref[...]], axis=0).astype(jnp.float32)
    out_ref[:, : query_ref.shape[1]] = query_ref[...]
    out_ref[:, query_ref.shape[1] :] = turned.T.astype(jnp.bfloat16)


def merge_kernel(low_ref, high_ref, weight_ref, place_ref, partial_ref, embed_ref, hold_ref):
    split, total = low_ref.shape[1], weight_ref.shape[1]
    chunks, chunk, _ = partial_ref.shape
    hold_ref[:split] = low_ref[3].astype(jnp.float32)
    hold_ref[split:] = high_ref[3].astype(jnp.float32)
    embed_ref[...] = jnp.zeros_like(embed_ref)
    for half in range(2):
        first, second = hold_ref[pl.ds(half * chunk, chunk), :], hold_ref[pl.ds((2 + half) * chunk, chunk), :]
        block = jnp.where(place_ref[0] == 0, first, second).astype(jnp.bfloat16)
        for i in range(chunks):
            embed_ref[2 * i + half, :chunk] = block
    acc = None
    for k in range(3):
        for ref, rows in ((low_ref, slice(0, split)), (high_ref, slice(split, total))):
            term = lax.dot_general(weight_ref[k, rows, :], ref[k], DIM0, preferred_element_type=jnp.float32)
            acc = term if acc is None else acc + term
    hold_ref[...] = acc
    for i in range(chunks):
        partial_ref[i] = hold_ref[pl.ds(i * chunk, chunk), :]


def settle_kernel(parts_ref, out_ref):
    total = parts_ref[0]
    for i in range(1, parts_ref.shape[0]):
        total = total + parts_ref[i]
    out_ref[...] = jnp.zeros_like(out_ref)
    out_ref[: parts_ref.shape[1]] = total.astype(jnp.bfloat16)


def spread_kernel(block_ref, out_ref):
    count = block_ref.shape[0]
    for i in range(out_ref.shape[0] // count):
        out_ref[i * count : (i + 1) * count] = block_ref[...]


def norm_kernel(embed_own, embed_other, merged_own, merged_other, place_ref, out_ref):
    core = place_ref[0]
    chunks = embed_own.shape[0]
    chunk = out_ref.shape[1]
    width = 2 * chunks * chunk
    for kind, pair in enumerate(((embed_own, embed_other), (merged_own, merged_other))):
        total = jnp.zeros((1, out_ref.shape[2]), jnp.float32)
        for ref in pair:
            for i in range(chunks):
                part = ref[i, :chunk].astype(jnp.float32)
                total = total + jnp.sum(part * part, axis=0, keepdims=True)
        scale = lax.rsqrt(total / width + 1e-06)
        for ref, side in zip(pair, (core, 1 - core)):
            for i in range(chunks):
                if kind == 0:
                    at = i // 2 * 4 + 2 * side + i % 2
                else:
                    at = 2 * chunks + (2 * (i % 2) + side) * 4 + i // 2
                out_ref[at] = (ref[i, :chunk].astype(jnp.float32) * scale).astype(jnp.bfloat16)


def project_columns(rows_ref, weights_hbm, first, weights_ref, arrived):
    pieces = arrived.shape[0]
    count, columns = weights_ref.shape[0] // pieces, weights_ref.shape[2]
    copies = []
    for p in range(pieces):
        span = pl.ds(p * count, count)
        source = weights_hbm.at[span, :, pl.ds(first, columns)]
        copies.append(pltpu.make_async_copy(source, weights_ref.at[span], arrived.at[p]))
        copies[-1].start()
    acc = jnp.zeros((columns, rows_ref.shape[2]), jnp.float32)
    for p in range(pieces):
        copies[p].wait()
        for at in range(p * count, (p + 1) * count):
            acc = acc + lax.dot_general(weights_ref[at], rows_ref[at], DIM0, preferred_element_type=jnp.float32)
    return acc


def project_kv_kernel(rows_ref, weights_hbm, place_ref, sent_ref, own_ref, weights_ref, arrived):
    x_id = place_ref[1]
    rows = project_columns(rows_ref, weights_hbm, 2 * HD, weights_ref, arrived).T.astype(jnp.bfloat16)
    size = own_ref.shape[0]
    quarter = rows[:size]
    for i in range(1, rows.shape[0] // size):
        quarter = jnp.where(x_id == i, rows[i * size : (i + 1) * size], quarter)
    for i in range(sent_ref.shape[0]):
        sent_ref[i] = quarter
    own_ref[...] = quarter


def project_q_kernel(rows_ref, weights_hbm, after_ref, query_ref, weights_ref, arrived):
    query_ref[...] = project_columns(rows_ref, weights_hbm, 0, weights_ref, arrived).astype(jnp.bfloat16)


def heads_of(query_ref, source):
    zeros = jnp.zeros((HD, BLK), jnp.bfloat16)
    pieces = []
    for a in range(2):
        for g in range(2):
            piece = query_ref[source, g * HD : (g + 1) * HD, a * BLK : (a + 1) * BLK]
            pieces.append(jnp.concatenate([piece * jnp.bfloat16(0.125), zeros], axis=0))
    return jnp.concatenate(pieces, axis=1)


def attend_keys(queries, keys_ref, bias_ref, state):
    top, total, accum = state
    groups, chunk, _ = keys_ref.shape
    keys = keys_ref[...].reshape(groups * chunk, 2 * HD)
    bias = bias_ref[...]
    scores = jnp.dot(keys, queries, preferred_element_type=jnp.float32)
    scores = scores.reshape(groups, chunk, queries.shape[1])
    highest = jnp.max(scores, axis=1) + bias
    new_top = jnp.maximum(top, jnp.max(highest, axis=0, keepdims=True))
    weights = jnp.exp(scores + (bias - new_top)[:, None, :])
    rescale = jnp.exp(top - new_top)
    weights = weights.reshape(groups * chunk, queries.shape[1])
    total = total * rescale + jnp.sum(weights, axis=0, keepdims=True)
    mixed = lax.dot_general(keys, weights.astype(jnp.bfloat16), DIM0, preferred_element_type=jnp.float32)
    return new_top, total, accum * rescale + mixed[HD:]


def store_state(out_ref, source, state):
    top, total, accum = state
    out_ref[source, :HD] = accum
    row = lax.broadcasted_iota(jnp.int32, (8, accum.shape[1]), 0)
    out_ref[source, HD:] = jnp.where(row == 0, top, total)


def own_kernel(query_ref, own_ref, place_ref, out_ref):
    x_id = place_ref[1]
    own = own_ref[...]
    chunk = own.shape[0]
    lanes = out_ref.shape[2]
    key_row = lax.broadcasted_iota(jnp.int32, (chunk, lanes), 0) + (x_id % 2) * chunk
    lane = lax.broadcasted_iota(jnp.int32, (chunk, lanes), 1)
    own_bias = jnp.where((lane // (2 * BLK) == x_id // 2) & (key_row <= lane % BLK), 0.0, -1e30)
    for source in range(query_ref.shape[0]):
        queries = heads_of(query_ref, source)
        scores = jnp.dot(own, queries, preferred_element_type=jnp.float32) + own_bias
        top = jnp.maximum(jnp.max(scores, axis=0, keepdims=True), -1e20)
        weights = jnp.exp(scores - top)
        total = jnp.sum(weights, axis=0, keepdims=True)
        accum = lax.dot_general(own, weights.astype(jnp.bfloat16), DIM0, preferred_element_type=jnp.float32)
        store_state(out_ref, source, (top, total, accum[HD:]))


def more_kernel(query_ref, keys_ref, bias_ref, state_ref, out_ref):
    for source in range(query_ref.shape[0]):
        state = (
            state_ref[source, HD : HD + 1, :],
            state_ref[source, HD + 1 : HD + 2, :],
            state_ref[source, :HD, :],
        )
        store_state(out_ref, source, attend_keys(heads_of(query_ref, source), keys_ref, bias_ref, state))


def combine_kernel(parts_ref, out_ref):
    count = parts_ref.shape[0]
    tops = [parts_ref[i, HD : HD + 1, :] for i in range(count)]
    top = tops[0]
    for i in range(1, count):
        top = jnp.maximum(top, tops[i])
    total = jnp.zeros_like(top)
    accum = jnp.zeros((HD, parts_ref.shape[2]), jnp.float32)
    for i in range(count):
        share = jnp.exp(tops[i] - top)
        total = total + parts_ref[i, HD + 1 : HD + 2, :] * share
        accum = accum + parts_ref[i, :HD, :] * share
    result = accum / total
    for a in range(2):
        left = result[:, 2 * a * BLK : (2 * a + 1) * BLK]
        right = result[:, (2 * a + 1) * BLK : (2 * a + 2) * BLK]
        out_ref[a * BLK : (a + 1) * BLK, :] = jnp.concatenate([left, right], axis=0).T.astype(jnp.bfloat16)


def body(hidden, merge_weight, query_weight, key_weight, value_weight, block_order):
    tokens, features = hidden.shape[1:]
    n_x, n_seg = lax.axis_size("x"), lax.axis_size(SEG)
    n_ctx = lax.axis_size(CTX)
    x_id, core, ctx_id = lax.axis_index("x"), lax.axis_index("core"), lax.axis_index(CTX)
    chunk = features // n_seg
    smem, hbm = pl.BlockSpec(memory_space=pltpu.SMEM), pl.BlockSpec(memory_space=pltpu.HBM)
    place = jnp.stack([core, x_id]).astype(jnp.int32)

    packed = pl.pallas_call(
        pack_kernel,
        out_shape=jax.ShapeDtypeStruct((query_weight.shape[0], 4 * HD), jnp.bfloat16),
        in_specs=[VMEM] * 3,
        out_specs=VMEM,
        name="pack",
    )(query_weight, key_weight.T, value_weight.T)
    weights = lax.all_gather(packed, "yh", axis=0)
    weights = lax.all_gather(weights, "z", axis=0)
    weights = weights.reshape(n_ctx, *weights.shape[2:])

    turned = hidden[0].T
    split = (features // 2 + 15) // 16 * 16
    low = lax.all_gather(turned[:split], SEG, axis=0)
    high = lax.all_gather(turned[split:], SEG, axis=0)

    padded = (chunk + 7) // 8 * 8
    partial, embed = pl.pallas_call(
        merge_kernel,
        out_shape=(
            jax.ShapeDtypeStruct((n_x, chunk, tokens), jnp.float32),
            jax.ShapeDtypeStruct((2 * n_x, padded, tokens), jnp.bfloat16),
        ),
        in_specs=[VMEM] * 3 + [smem],
        out_specs=(VMEM, VMEM),
        scratch_shapes=[pltpu.VMEM((features, tokens), jnp.float32)],
        compiler_params=pltpu.CompilerParams(vmem_limit_bytes=40 << 20),
        name="merge",
    )(low, high, merge_weight, place)
    parts = lax.all_to_all(partial, "x", 0, 0)
    merged = pl.pallas_call(
        settle_kernel,
        out_shape=jax.ShapeDtypeStruct((padded, tokens), jnp.bfloat16),
        in_specs=[VMEM],
        out_specs=VMEM,
        name="settle",
    )(parts)
    merged = lax.all_gather(merged, "yl", axis=0)
    merged = pl.pallas_call(
        spread_kernel,
        out_shape=jax.ShapeDtypeStruct((2 * n_x, padded, tokens), jnp.bfloat16),
        in_specs=[VMEM],
        out_specs=VMEM,
        name="spread",
    )(merged)

    def over_x(copies):
        own = lax.all_to_all(copies, "x", 0, 0, tiled=True)
        return own, lax.ppermute(own, "core", [(0, 1), (1, 0)])

    embed_own, embed_other = over_x(embed)
    merged_own, merged_other = over_x(merged)

    quarter = tokens // n_x
    params = pltpu.CompilerParams(vmem_limit_bytes=40 << 20)
    rows = pl.pallas_call(
        norm_kernel,
        out_shape=jax.ShapeDtypeStruct((n_ctx, chunk, tokens), jnp.bfloat16),
        in_specs=[VMEM] * 4 + [smem],
        out_specs=VMEM,
        compiler_params=params,
        name="norm",
    )(embed_own, embed_other, merged_own, merged_other, place)
    n_z, n_yh = lax.axis_size("z"), lax.axis_size("yh")
    tight = pltpu.CompilerParams(vmem_limit_bytes=50 << 20)
    scratch = [pltpu.VMEM((n_ctx, chunk, 2 * HD), jnp.bfloat16), pltpu.SemaphoreType.DMA((4,))]
    sent, own = pl.pallas_call(
        project_kv_kernel,
        out_shape=(
            jax.ShapeDtypeStruct((n_z, quarter, 2 * HD), jnp.bfloat16),
            jax.ShapeDtypeStruct((quarter, 2 * HD), jnp.bfloat16),
        ),
        in_specs=[VMEM, hbm, smem],
        out_specs=(VMEM, VMEM),
        scratch_shapes=scratch,
        compiler_params=tight,
        name="project_kv",
    )(rows, weights, place)
    taken = lax.all_to_all(sent, "z", 0, 0)
    query = pl.pallas_call(
        project_q_kernel,
        out_shape=jax.ShapeDtypeStruct((2 * HD, tokens), jnp.bfloat16),
        in_specs=[VMEM, hbm, VMEM],
        out_specs=VMEM,
        scratch_shapes=scratch,
        compiler_params=tight,
        name="project_q",
    )(rows, weights, own)
    queries = lax.all_gather(query, "x", axis=0)
    state = jax.ShapeDtypeStruct((n_x, HD + 8, 4 * BLK), jnp.float32)
    parts = pl.pallas_call(
        own_kernel,
        out_shape=state,
        in_specs=[VMEM] * 2 + [smem],
        out_specs=VMEM,
        compiler_params=params,
        name="attend_own",
    )(queries, own, place)
    taken, queries, parts = lax.optimization_barrier((taken, queries, parts))
    other = lax.ppermute(taken, "yh", [(0, 1), (1, 0)])

    placed = block_order.reshape(n_z, n_yh, 2)
    placed = jnp.where(x_id < n_x // 2, placed[:, :, 0], placed[:, :, 1])
    mine = jnp.repeat(lax.dynamic_slice_in_dim(block_order, ctx_id * 2, 2, 0), 2 * BLK)
    yh = lax.axis_index("yh")
    near = jnp.where(yh == 0, placed[:, 0], placed[:, 1])
    far = jnp.where(yh == 0, placed[:, 1], placed[:, 0])
    near = jnp.where(near[:, None] < mine[None, :], 0.0, -1e30).astype(jnp.float32)
    far = jnp.where(far[:, None] < mine[None, :], 0.0, -1e30).astype(jnp.float32)

    scores = 8 * BLK * 2 * n_z * quarter
    cost = pl.CostEstimate(flops=scores * 4 * HD, bytes_accessed=2 << 20, transcendentals=scores)
    for keys, bias in ((taken, near), (other, far)):
        parts = pl.pallas_call(
            more_kernel,
            out_shape=state,
            in_specs=[VMEM] * 4,
            out_specs=VMEM,
            compiler_params=params,
            cost_estimate=cost,
            name="attend_more",
        )(queries, keys, bias, parts)
    parts = lax.all_to_all(parts, "x", 0, 0)
    return pl.pallas_call(
        combine_kernel,
        out_shape=jax.ShapeDtypeStruct((tokens, 2 * HD), jnp.bfloat16),
        in_specs=[VMEM],
        out_specs=VMEM,
        name="combine",
    )(parts)


def solution(mesh):
    shape = mesh.shape
    grid = mesh.devices.reshape(2, shape["segment"] // 2, shape["ctx"] // 2, 2, shape["head"])
    fine = Mesh(grid, ("yl", "core", "z", "yh", "x"))
    return jax.shard_map(
        body,
        mesh=fine,
        in_specs=(
            P(SEG, CTX, "x"),
            P(None, "x", SEG),
            P(CTX, (*SEG, "x")),
            P(CTX, SEG),
            P(CTX, SEG),
            P(),
        ),
        out_specs=P(CTX, (*SEG, "x")),
        check_vma=False,
    )
```

```python
import jax
import jax.numpy as jnp
from jax import lax
from jax.experimental import pallas as pl
from jax.experimental.pallas import tpu as pltpu
from jax.sharding import Mesh, PartitionSpec as P

HD = 64
BLK = 128
SEG = ("yl", "core")
CTX = ("z", "yh")
VMEM = pl.BlockSpec(memory_space=pltpu.VMEM)
DIM0 = (((0,), (0,)), ((), ()))


def pack_kernel(query_ref, key_ref, value_ref, out_ref):
    turned = jnp.concatenate([key_ref[...], value_ref[...]], axis=0).astype(jnp.float32)
    chunk = query_ref.shape[0]
    out_ref[...] = jnp.zeros_like(out_ref)
    out_ref[:chunk, : query_ref.shape[1]] = query_ref[...]
    out_ref[:chunk, query_ref.shape[1] :] = turned.T.astype(jnp.bfloat16)


def merge_kernel(low_ref, high_ref, weight_ref, place_ref, partial_ref, embed_ref, hold_ref):
    split, total = low_ref.shape[1], weight_ref.shape[1]
    chunks, chunk, _ = partial_ref.shape
    hold_ref[:split] = low_ref[3].astype(jnp.float32)
    hold_ref[split:] = high_ref[3].astype(jnp.float32)
    embed_ref[...] = jnp.zeros_like(embed_ref)
    for half in range(2):
        first, second = hold_ref[pl.ds(half * chunk, chunk), :], hold_ref[pl.ds((2 + half) * chunk, chunk), :]
        block = jnp.where(place_ref[0] == 0, first, second).astype(jnp.bfloat16)
        for i in range(chunks):
            embed_ref[2 * i + half, :chunk] = block
    acc = None
    for k in range(3):
        for ref, rows in ((low_ref, slice(0, split)), (high_ref, slice(split, total))):
            term = lax.dot_general(weight_ref[k, rows, :], ref[k], DIM0, preferred_element_type=jnp.float32)
            acc = term if acc is None else acc + term
    hold_ref[...] = acc
    for i in range(chunks):
        partial_ref[i] = hold_ref[pl.ds(i * chunk, chunk), :]


def settle_kernel(parts_ref, out_ref):
    total = parts_ref[0]
    for i in range(1, parts_ref.shape[0]):
        total = total + parts_ref[i]
    out_ref[...] = jnp.zeros_like(out_ref)
    out_ref[: parts_ref.shape[1]] = total.astype(jnp.bfloat16)


def spread_kernel(block_ref, out_ref):
    count = block_ref.shape[0]
    for i in range(out_ref.shape[0] // count):
        out_ref[i * count : (i + 1) * count] = block_ref[...]


def project_kernel(
    embed_own, embed_other, merged_own, merged_other, weights_hbm, place_ref,
    query_ref, sent_ref, own_ref, rows_ref, weights_ref, arrived,
):
    core, x_id = place_ref[0], place_ref[1]
    pieces = arrived.shape[0]
    count = weights_ref.shape[0] // pieces
    copies = []
    for p in range(pieces):
        span = pl.ds(p * count, count)
        copies.append(pltpu.make_async_copy(weights_hbm.at[span], weights_ref.at[span], arrived.at[p]))
        copies[-1].start()
    chunks = embed_own.shape[0]
    _, chunk, tokens = rows_ref.shape
    width = 2 * chunks * chunk
    for kind, pair in enumerate(((embed_own, embed_other), (merged_own, merged_other))):
        total = jnp.zeros((1, tokens), jnp.float32)
        for ref in pair:
            for i in range(chunks):
                part = ref[i, :chunk].astype(jnp.float32)
                total = total + jnp.sum(part * part, axis=0, keepdims=True)
        scale = lax.rsqrt(total / width + 1e-06)
        for ref, side in zip(pair, (core, 1 - core)):
            for i in range(chunks):
                if kind == 0:
                    at = i // 2 * 4 + 2 * side + i % 2
                else:
                    at = 2 * chunks + (2 * (i % 2) + side) * 4 + i // 2
                rows_ref[at] = (ref[i, :chunk].astype(jnp.float32) * scale).astype(jnp.bfloat16)
    acc = jnp.zeros((weights_ref.shape[2], tokens), jnp.float32)
    for p in range(pieces):
        copies[p].wait()
        for at in range(p * count, (p + 1) * count):
            acc = acc + lax.dot_general(
                weights_ref[at, :chunk], rows_ref[at], DIM0, preferred_element_type=jnp.float32
            )
    half = acc.shape[0] // 2
    query_ref[...] = acc[:half].astype(jnp.bfloat16)
    rows = acc[half:].T.astype(jnp.bfloat16)
    size = own_ref.shape[0]
    quarter = rows[:size]
    for i in range(1, tokens // size):
        quarter = jnp.where(x_id == i, rows[i * size : (i + 1) * size], quarter)
    for i in range(sent_ref.shape[0]):
        sent_ref[i] = quarter
    own_ref[...] = quarter


def heads_of(query_ref, source):
    zeros = jnp.zeros((HD, BLK), jnp.bfloat16)
    pieces = []
    for a in range(2):
        for g in range(2):
            piece = query_ref[source, g * HD : (g + 1) * HD, a * BLK : (a + 1) * BLK]
            pieces.append(jnp.concatenate([piece * jnp.bfloat16(0.125), zeros], axis=0))
    return jnp.concatenate(pieces, axis=1)


def attend_keys(queries, keys_ref, bias_ref, state):
    top, total, accum = state
    groups, chunk, _ = keys_ref.shape
    keys = keys_ref[...].reshape(groups * chunk, 2 * HD)
    bias = bias_ref[...]
    scores = jnp.dot(keys, queries, preferred_element_type=jnp.float32)
    scores = scores.reshape(groups, chunk, queries.shape[1])
    highest = jnp.max(scores, axis=1) + bias
    new_top = jnp.maximum(top, jnp.max(highest, axis=0, keepdims=True))
    weights = jnp.exp(scores + (bias - new_top)[:, None, :])
    rescale = jnp.exp(top - new_top)
    weights = weights.reshape(groups * chunk, queries.shape[1])
    total = total * rescale + jnp.sum(weights, axis=0, keepdims=True)
    mixed = lax.dot_general(keys, weights.astype(jnp.bfloat16), DIM0, preferred_element_type=jnp.float32)
    return new_top, total, accum * rescale + mixed[HD:]


def store_state(out_ref, source, state):
    top, total, accum = state
    out_ref[source, :HD] = accum
    row = lax.broadcasted_iota(jnp.int32, (8, accum.shape[1]), 0)
    out_ref[source, HD:] = jnp.where(row == 0, top, total)


def own_kernel(query_ref, own_ref, place_ref, out_ref):
    x_id = place_ref[1]
    own = own_ref[...]
    chunk = own.shape[0]
    lanes = out_ref.shape[2]
    key_row = lax.broadcasted_iota(jnp.int32, (chunk, lanes), 0) + (x_id % 2) * chunk
    lane = lax.broadcasted_iota(jnp.int32, (chunk, lanes), 1)
    own_bias = jnp.where((lane // (2 * BLK) == x_id // 2) & (key_row <= lane % BLK), 0.0, -1e30)
    for source in range(query_ref.shape[0]):
        queries = heads_of(query_ref, source)
        scores = jnp.dot(own, queries, preferred_element_type=jnp.float32) + own_bias
        top = jnp.maximum(jnp.max(scores, axis=0, keepdims=True), -1e20)
        weights = jnp.exp(scores - top)
        total = jnp.sum(weights, axis=0, keepdims=True)
        accum = lax.dot_general(own, weights.astype(jnp.bfloat16), DIM0, preferred_element_type=jnp.float32)
        store_state(out_ref, source, (top, total, accum[HD:]))


def load_state(state_ref, source):
    rows = (slice(HD, HD + 1), slice(HD + 1, HD + 2), slice(0, HD))
    return tuple(state_ref[source, r, :] for r in rows)


def more_kernel(query_ref, keys_ref, bias_ref, state_ref, out_ref):
    for source in range(query_ref.shape[0]):
        state = load_state(state_ref, source)
        store_state(out_ref, source, attend_keys(heads_of(query_ref, source), keys_ref, bias_ref, state))


def thirds(value):
    high = value.astype(jnp.bfloat16).astype(jnp.float32)
    middle = (value - high).astype(jnp.bfloat16).astype(jnp.float32)
    return high, middle, value - high - middle


def last_kernel(query_ref, keys_ref, bias_ref, state_ref, out_ref):
    for source in range(query_ref.shape[0]):
        top, total, accum = attend_keys(
            heads_of(query_ref, source), keys_ref, bias_ref, load_state(state_ref, source)
        )
        out_ref[source, :HD] = accum.astype(jnp.bfloat16)
        row = lax.broadcasted_iota(jnp.int32, (out_ref.shape[1] - HD, accum.shape[1]), 0)
        rest = jnp.zeros(row.shape, jnp.float32)
        for at, term in enumerate((*thirds(top), *thirds(total))):
            rest = jnp.where(row == at, term, rest)
        out_ref[source, HD:] = rest.astype(jnp.bfloat16)


def combine_kernel(parts_ref, out_ref):
    count = parts_ref.shape[0]
    tops, totals = [], []
    for i in range(count):
        rest = parts_ref[i, HD:, :].astype(jnp.float32)
        tops.append(rest[0:1] + rest[1:2] + rest[2:3])
        totals.append(rest[3:4] + rest[4:5] + rest[5:6])
    top = tops[0]
    for i in range(1, count):
        top = jnp.maximum(top, tops[i])
    total = jnp.zeros_like(top)
    accum = jnp.zeros((HD, parts_ref.shape[2]), jnp.float32)
    for i in range(count):
        share = jnp.exp(tops[i] - top)
        total = total + totals[i] * share
        accum = accum + parts_ref[i, :HD, :].astype(jnp.float32) * share
    result = accum / total
    for a in range(2):
        left = result[:, 2 * a * BLK : (2 * a + 1) * BLK]
        right = result[:, (2 * a + 1) * BLK : (2 * a + 2) * BLK]
        out_ref[a * BLK : (a + 1) * BLK, :] = jnp.concatenate([left, right], axis=0).T.astype(jnp.bfloat16)


def body(hidden, merge_weight, query_weight, key_weight, value_weight, block_order):
    tokens, features = hidden.shape[1:]
    n_x, n_seg = lax.axis_size("x"), lax.axis_size(SEG)
    n_ctx = lax.axis_size(CTX)
    x_id, core, ctx_id = lax.axis_index("x"), lax.axis_index("core"), lax.axis_index(CTX)
    chunk = features // n_seg
    smem, hbm = pl.BlockSpec(memory_space=pltpu.SMEM), pl.BlockSpec(memory_space=pltpu.HBM)
    place = jnp.stack([core, x_id]).astype(jnp.int32)

    padded = (chunk + 7) // 8 * 8
    packed = pl.pallas_call(
        pack_kernel,
        out_shape=jax.ShapeDtypeStruct((padded, 4 * HD), jnp.bfloat16),
        in_specs=[VMEM] * 3,
        out_specs=VMEM,
        name="pack",
    )(query_weight, key_weight.T, value_weight.T)
    weights = lax.all_gather(packed, "yh", axis=0)
    weights = lax.all_gather(weights, "z", axis=0)
    weights = weights.reshape(n_ctx, *weights.shape[2:])

    turned = hidden[0].T
    split = (features // 2 + 15) // 16 * 16
    low = lax.all_gather(turned[:split], SEG, axis=0)
    high = lax.all_gather(turned[split:], SEG, axis=0)

    partial, embed = pl.pallas_call(
        merge_kernel,
        out_shape=(
            jax.ShapeDtypeStruct((n_x, chunk, tokens), jnp.float32),
            jax.ShapeDtypeStruct((2 * n_x, padded, tokens), jnp.bfloat16),
        ),
        in_specs=[VMEM] * 3 + [smem],
        out_specs=(VMEM, VMEM),
        scratch_shapes=[pltpu.VMEM((features, tokens), jnp.float32)],
        compiler_params=pltpu.CompilerParams(vmem_limit_bytes=40 << 20),
        name="merge",
    )(low, high, merge_weight, place)
    parts = lax.all_to_all(partial, "x", 0, 0)
    merged = pl.pallas_call(
        settle_kernel,
        out_shape=jax.ShapeDtypeStruct((padded, tokens), jnp.bfloat16),
        in_specs=[VMEM],
        out_specs=VMEM,
        name="settle",
    )(parts)
    merged = lax.all_gather(merged, "yl", axis=0)
    merged = pl.pallas_call(
        spread_kernel,
        out_shape=jax.ShapeDtypeStruct((2 * n_x, padded, tokens), jnp.bfloat16),
        in_specs=[VMEM],
        out_specs=VMEM,
        name="spread",
    )(merged)

    def over_x(copies):
        own = lax.all_to_all(copies, "x", 0, 0, tiled=True)
        return own, lax.ppermute(own, "core", [(0, 1), (1, 0)])

    embed_own, embed_other = over_x(embed)
    merged_own, merged_other = over_x(merged)

    quarter = tokens // n_x
    params = pltpu.CompilerParams(vmem_limit_bytes=40 << 20)
    n_z, n_yh = lax.axis_size("z"), lax.axis_size("yh")
    query, sent, own = pl.pallas_call(
        project_kernel,
        out_shape=(
            jax.ShapeDtypeStruct((2 * HD, tokens), jnp.bfloat16),
            jax.ShapeDtypeStruct((n_z, quarter, 2 * HD), jnp.bfloat16),
            jax.ShapeDtypeStruct((quarter, 2 * HD), jnp.bfloat16),
        ),
        in_specs=[VMEM] * 4 + [hbm, smem],
        out_specs=(VMEM, VMEM, VMEM),
        scratch_shapes=[
            pltpu.VMEM((n_ctx, chunk, tokens), jnp.bfloat16),
            pltpu.VMEM(weights.shape, weights.dtype),
            pltpu.SemaphoreType.DMA((4,)),
        ],
        compiler_params=pltpu.CompilerParams(vmem_limit_bytes=48 << 20),
        name="project",
    )(embed_own, embed_other, merged_own, merged_other, weights, place)
    taken = lax.all_to_all(sent, "z", 0, 0)
    queries = lax.all_gather(query, "x", axis=0)
    state = jax.ShapeDtypeStruct((n_x, HD + 8, 4 * BLK), jnp.float32)
    parts = pl.pallas_call(
        own_kernel,
        out_shape=state,
        in_specs=[VMEM] * 2 + [smem],
        out_specs=VMEM,
        compiler_params=params,
        name="attend_own",
    )(queries, own, place)
    taken, queries, parts = lax.optimization_barrier((taken, queries, parts))
    other = lax.ppermute(taken, "yh", [(0, 1), (1, 0)])

    placed = block_order.reshape(n_z, n_yh, 2)
    placed = jnp.where(x_id < n_x // 2, placed[:, :, 0], placed[:, :, 1])
    mine = jnp.repeat(lax.dynamic_slice_in_dim(block_order, ctx_id * 2, 2, 0), 2 * BLK)
    yh = lax.axis_index("yh")
    near = jnp.where(yh == 0, placed[:, 0], placed[:, 1])
    far = jnp.where(yh == 0, placed[:, 1], placed[:, 0])
    near = jnp.where(near[:, None] < mine[None, :], 0.0, -1e30).astype(jnp.float32)
    far = jnp.where(far[:, None] < mine[None, :], 0.0, -1e30).astype(jnp.float32)

    scores = 8 * BLK * 2 * n_z * quarter
    cost = pl.CostEstimate(flops=scores * 4 * HD, bytes_accessed=2 << 20, transcendentals=scores)
    sums = jax.ShapeDtypeStruct((n_x, HD + 16, 4 * BLK), jnp.bfloat16)
    for kernel, keys, bias, shape in ((more_kernel, taken, near, state), (last_kernel, other, far, sums)):
        parts = pl.pallas_call(
            kernel,
            out_shape=shape,
            in_specs=[VMEM] * 4,
            out_specs=VMEM,
            compiler_params=params,
            cost_estimate=cost,
            name="attend_more",
        )(queries, keys, bias, parts)
    parts = lax.all_to_all(parts, "x", 0, 0)
    return pl.pallas_call(
        combine_kernel,
        out_shape=jax.ShapeDtypeStruct((tokens, 2 * HD), jnp.bfloat16),
        in_specs=[VMEM],
        out_specs=VMEM,
        name="combine",
    )(parts)


def solution(mesh):
    shape = mesh.shape
    grid = mesh.devices.reshape(2, shape["segment"] // 2, shape["ctx"] // 2, 2, shape["head"])
    fine = Mesh(grid, ("yl", "core", "z", "yh", "x"))
    return jax.shard_map(
        body,
        mesh=fine,
        in_specs=(
            P(SEG, CTX, "x"),
            P(None, "x", SEG),
            P(CTX, (*SEG, "x")),
            P(CTX, SEG),
            P(CTX, SEG),
            P(),
        ),
        out_specs=P(CTX, (*SEG, "x")),
        check_vma=False,
    )
```

```python
import jax
import jax.numpy as jnp
from jax import lax
from jax.experimental import pallas as pl
from jax.experimental.pallas import tpu as pltpu
from jax.sharding import Mesh, PartitionSpec as P

HD = 64
BLK = 128
SEG = ("yl", "core")
CTX = ("z", "yh")
VMEM = pl.BlockSpec(memory_space=pltpu.VMEM)
DIM0 = (((0,), (0,)), ((), ()))


def pack_kernel(query_ref, key_ref, value_ref, out_ref):
    turned = jnp.concatenate([key_ref[...], value_ref[...]], axis=0).astype(jnp.float32)
    chunk = query_ref.shape[0]
    out_ref[...] = jnp.zeros_like(out_ref)
    out_ref[:chunk, : query_ref.shape[1]] = query_ref[...]
    out_ref[:chunk, query_ref.shape[1] :] = turned.T.astype(jnp.bfloat16)


def merge_kernel(low_ref, high_ref, weight_ref, place_ref, partial_ref, embed_ref, hold_ref):
    split, total = low_ref.shape[1], weight_ref.shape[1]
    chunks, chunk, _ = partial_ref.shape
    hold_ref[:split] = low_ref[3].astype(jnp.float32)
    hold_ref[split:] = high_ref[3].astype(jnp.float32)
    embed_ref[...] = jnp.zeros_like(embed_ref)
    for half in range(2):
        first, second = hold_ref[pl.ds(half * chunk, chunk), :], hold_ref[pl.ds((2 + half) * chunk, chunk), :]
        block = jnp.where(place_ref[0] == 0, first, second).astype(jnp.bfloat16)
        for i in range(chunks):
            embed_ref[2 * i + half, :chunk] = block
    acc = None
    for k in range(3):
        for ref, rows in ((low_ref, slice(0, split)), (high_ref, slice(split, total))):
            term = lax.dot_general(weight_ref[k, rows, :], ref[k], DIM0, preferred_element_type=jnp.float32)
            acc = term if acc is None else acc + term
    hold_ref[...] = acc
    for i in range(chunks):
        partial_ref[i] = hold_ref[pl.ds(i * chunk, chunk), :]


def settle_kernel(parts_ref, out_ref):
    total = parts_ref[0]
    for i in range(1, parts_ref.shape[0]):
        total = total + parts_ref[i]
    out_ref[...] = jnp.zeros_like(out_ref)
    out_ref[: parts_ref.shape[1]] = total.astype(jnp.bfloat16)


def spread_kernel(block_ref, out_ref):
    count = block_ref.shape[0]
    for i in range(out_ref.shape[0] // count):
        out_ref[i * count : (i + 1) * count] = block_ref[...]


def project_kernel(
    embed_own, embed_other, merged_own, merged_other, weights_hbm, place_ref,
    query_ref, sent_ref, own_ref, rows_ref, weights_ref, arrived,
):
    core, x_id = place_ref[0], place_ref[1]
    copy = pltpu.make_async_copy(weights_hbm, weights_ref, arrived)
    copy.start()
    chunks = embed_own.shape[0]
    _, chunk, tokens = rows_ref.shape
    width = 2 * chunks * chunk
    for kind, pair in enumerate(((embed_own, embed_other), (merged_own, merged_other))):
        total = jnp.zeros((1, tokens), jnp.float32)
        for ref in pair:
            for i in range(chunks):
                part = ref[i, :chunk].astype(jnp.float32)
                total = total + jnp.sum(part * part, axis=0, keepdims=True)
        scale = lax.rsqrt(total / width + 1e-06)
        for ref, side in zip(pair, (core, 1 - core)):
            for i in range(chunks):
                if kind == 0:
                    at = i // 2 * 4 + 2 * side + i % 2
                else:
                    at = 2 * chunks + (2 * (i % 2) + side) * 4 + i // 2
                rows_ref[at] = (ref[i, :chunk].astype(jnp.float32) * scale).astype(jnp.bfloat16)
    acc = jnp.zeros((weights_ref.shape[2], tokens), jnp.float32)
    copy.wait()
    for at in range(weights_ref.shape[0]):
        acc = acc + lax.dot_general(
            weights_ref[at, :chunk], rows_ref[at], DIM0, preferred_element_type=jnp.float32
        )
    half = acc.shape[0] // 2
    query_ref[...] = acc[:half].astype(jnp.bfloat16)
    rows = acc[half:].T.astype(jnp.bfloat16)
    size = own_ref.shape[0]
    quarter = rows[:size]
    for i in range(1, tokens // size):
        quarter = jnp.where(x_id == i, rows[i * size : (i + 1) * size], quarter)
    for i in range(sent_ref.shape[0]):
        sent_ref[i] = quarter
    own_ref[...] = quarter


def heads_of(query_ref, source):
    zeros = jnp.zeros((HD, BLK), jnp.bfloat16)
    pieces = []
    for a in range(2):
        for g in range(2):
            piece = query_ref[source, g * HD : (g + 1) * HD, a * BLK : (a + 1) * BLK]
            pieces.append(jnp.concatenate([piece * jnp.bfloat16(0.125), zeros], axis=0))
    return jnp.concatenate(pieces, axis=1)


def attend_keys(queries, keys_ref, bias_ref, state):
    top, total, accum = state
    groups, chunk, _ = keys_ref.shape
    keys = keys_ref[...].reshape(groups * chunk, 2 * HD)
    bias = bias_ref[...]
    scores = jnp.dot(keys, queries, preferred_element_type=jnp.float32)
    scores = scores.reshape(groups, chunk, queries.shape[1])
    highest = jnp.max(scores, axis=1) + bias
    new_top = jnp.maximum(top, jnp.max(highest, axis=0, keepdims=True))
    weights = jnp.exp(scores + (bias - new_top)[:, None, :])
    rescale = jnp.exp(top - new_top)
    weights = weights.reshape(groups * chunk, queries.shape[1])
    total = total * rescale + jnp.sum(weights, axis=0, keepdims=True)
    mixed = lax.dot_general(keys, weights.astype(jnp.bfloat16), DIM0, preferred_element_type=jnp.float32)
    return new_top, total, accum * rescale + mixed[HD:]


def store_state(out_ref, source, state):
    top, total, accum = state
    out_ref[source, :HD] = accum
    row = lax.broadcasted_iota(jnp.int32, (8, accum.shape[1]), 0)
    out_ref[source, HD:] = jnp.where(row == 0, top, total)


def own_kernel(query_ref, own_ref, place_ref, out_ref):
    x_id = place_ref[1]
    own = own_ref[...]
    chunk = own.shape[0]
    lanes = out_ref.shape[2]
    key_row = lax.broadcasted_iota(jnp.int32, (chunk, lanes), 0) + (x_id % 2) * chunk
    lane = lax.broadcasted_iota(jnp.int32, (chunk, lanes), 1)
    own_bias = jnp.where((lane // (2 * BLK) == x_id // 2) & (key_row <= lane % BLK), 0.0, -1e30)
    for source in range(query_ref.shape[0]):
        queries = heads_of(query_ref, source)
        scores = jnp.dot(own, queries, preferred_element_type=jnp.float32) + own_bias
        top = jnp.maximum(jnp.max(scores, axis=0, keepdims=True), -1e20)
        weights = jnp.exp(scores - top)
        total = jnp.sum(weights, axis=0, keepdims=True)
        accum = lax.dot_general(own, weights.astype(jnp.bfloat16), DIM0, preferred_element_type=jnp.float32)
        store_state(out_ref, source, (top, total, accum[HD:]))


def load_state(state_ref, source):
    rows = (slice(HD, HD + 1), slice(HD + 1, HD + 2), slice(0, HD))
    return tuple(state_ref[source, r, :] for r in rows)


def more_kernel(query_ref, keys_ref, bias_ref, state_ref, out_ref):
    for source in range(query_ref.shape[0]):
        state = load_state(state_ref, source)
        store_state(out_ref, source, attend_keys(heads_of(query_ref, source), keys_ref, bias_ref, state))


def thirds(value):
    high = value.astype(jnp.bfloat16).astype(jnp.float32)
    middle = (value - high).astype(jnp.bfloat16).astype(jnp.float32)
    return high, middle, value - high - middle


def last_kernel(query_ref, keys_ref, bias_ref, state_ref, out_ref):
    for source in range(query_ref.shape[0]):
        top, total, accum = attend_keys(
            heads_of(query_ref, source), keys_ref, bias_ref, load_state(state_ref, source)
        )
        out_ref[source, :HD] = accum.astype(jnp.bfloat16)
        row = lax.broadcasted_iota(jnp.int32, (out_ref.shape[1] - HD, accum.shape[1]), 0)
        rest = jnp.zeros(row.shape, jnp.float32)
        for at, term in enumerate((*thirds(top), *thirds(total))):
            rest = jnp.where(row == at, term, rest)
        out_ref[source, HD:] = rest.astype(jnp.bfloat16)


def combine_kernel(parts_ref, out_ref):
    count = parts_ref.shape[0]
    tops, totals = [], []
    for i in range(count):
        rest = parts_ref[i, HD:, :].astype(jnp.float32)
        tops.append(rest[0:1] + rest[1:2] + rest[2:3])
        totals.append(rest[3:4] + rest[4:5] + rest[5:6])
    top = tops[0]
    for i in range(1, count):
        top = jnp.maximum(top, tops[i])
    total = jnp.zeros_like(top)
    accum = jnp.zeros((HD, parts_ref.shape[2]), jnp.float32)
    for i in range(count):
        share = jnp.exp(tops[i] - top)
        total = total + totals[i] * share
        accum = accum + parts_ref[i, :HD, :].astype(jnp.float32) * share
    result = accum / total
    for a in range(2):
        left = result[:, 2 * a * BLK : (2 * a + 1) * BLK]
        right = result[:, (2 * a + 1) * BLK : (2 * a + 2) * BLK]
        out_ref[a * BLK : (a + 1) * BLK, :] = jnp.concatenate([left, right], axis=0).T.astype(jnp.bfloat16)


def body(hidden, merge_weight, query_weight, key_weight, value_weight, block_order):
    tokens, features = hidden.shape[1:]
    n_x, n_seg = lax.axis_size("x"), lax.axis_size(SEG)
    n_ctx = lax.axis_size(CTX)
    x_id, core, ctx_id = lax.axis_index("x"), lax.axis_index("core"), lax.axis_index(CTX)
    chunk = features // n_seg
    smem, hbm = pl.BlockSpec(memory_space=pltpu.SMEM), pl.BlockSpec(memory_space=pltpu.HBM)
    place = jnp.stack([core, x_id]).astype(jnp.int32)

    padded = (chunk + 7) // 8 * 8
    packed = pl.pallas_call(
        pack_kernel,
        out_shape=jax.ShapeDtypeStruct((padded, 4 * HD), jnp.bfloat16),
        in_specs=[VMEM] * 3,
        out_specs=VMEM,
        name="pack",
    )(query_weight, key_weight.T, value_weight.T)
    weights = lax.all_gather(packed, "yh", axis=0)
    weights = lax.all_gather(weights, "z", axis=0)
    weights = weights.reshape(n_ctx, *weights.shape[2:])

    turned = hidden[0].T
    split = (features // 2 + 15) // 16 * 16
    low = lax.all_gather(turned[:split], SEG, axis=0)
    high = lax.all_gather(turned[split:], SEG, axis=0)

    partial, embed = pl.pallas_call(
        merge_kernel,
        out_shape=(
            jax.ShapeDtypeStruct((n_x, chunk, tokens), jnp.float32),
            jax.ShapeDtypeStruct((2 * n_x, padded, tokens), jnp.bfloat16),
        ),
        in_specs=[VMEM] * 3 + [smem],
        out_specs=(VMEM, VMEM),
        scratch_shapes=[pltpu.VMEM((features, tokens), jnp.float32)],
        compiler_params=pltpu.CompilerParams(vmem_limit_bytes=40 << 20),
        name="merge",
    )(low, high, merge_weight, place)
    parts = lax.all_to_all(partial, "x", 0, 0)
    merged = pl.pallas_call(
        settle_kernel,
        out_shape=jax.ShapeDtypeStruct((padded, tokens), jnp.bfloat16),
        in_specs=[VMEM],
        out_specs=VMEM,
        name="settle",
    )(parts)
    merged = lax.all_gather(merged, "yl", axis=0)
    merged = pl.pallas_call(
        spread_kernel,
        out_shape=jax.ShapeDtypeStruct((2 * n_x, padded, tokens), jnp.bfloat16),
        in_specs=[VMEM],
        out_specs=VMEM,
        name="spread",
    )(merged)

    def over_x(copies):
        own = lax.all_to_all(copies, "x", 0, 0, tiled=True)
        return own, lax.ppermute(own, "core", [(0, 1), (1, 0)])

    embed_own, embed_other = over_x(embed)
    merged_own, merged_other = over_x(merged)

    quarter = tokens // n_x
    params = pltpu.CompilerParams(vmem_limit_bytes=40 << 20)
    n_z, n_yh = lax.axis_size("z"), lax.axis_size("yh")
    query, sent, own = pl.pallas_call(
        project_kernel,
        out_shape=(
            jax.ShapeDtypeStruct((2 * HD, tokens), jnp.bfloat16),
            jax.ShapeDtypeStruct((n_z, quarter, 2 * HD), jnp.bfloat16),
            jax.ShapeDtypeStruct((quarter, 2 * HD), jnp.bfloat16),
        ),
        in_specs=[VMEM] * 4 + [hbm, smem],
        out_specs=(VMEM, VMEM, VMEM),
        scratch_shapes=[
            pltpu.VMEM((n_ctx, chunk, tokens), jnp.bfloat16),
            pltpu.VMEM(weights.shape, weights.dtype),
            pltpu.SemaphoreType.DMA,
        ],
        compiler_params=pltpu.CompilerParams(vmem_limit_bytes=48 << 20),
        name="project",
    )(embed_own, embed_other, merged_own, merged_other, weights, place)
    taken = lax.all_to_all(sent, "z", 0, 0)
    queries = lax.all_gather(query, "x", axis=0)
    state = jax.ShapeDtypeStruct((n_x, HD + 8, 4 * BLK), jnp.float32)
    parts = pl.pallas_call(
        own_kernel,
        out_shape=state,
        in_specs=[VMEM] * 2 + [smem],
        out_specs=VMEM,
        compiler_params=params,
        name="attend_own",
    )(queries, own, place)
    taken, queries, parts = lax.optimization_barrier((taken, queries, parts))
    other = lax.ppermute(taken, "yh", [(0, 1), (1, 0)])

    placed = block_order.reshape(n_z, n_yh, 2)
    placed = jnp.where(x_id < n_x // 2, placed[:, :, 0], placed[:, :, 1])
    mine = jnp.repeat(lax.dynamic_slice_in_dim(block_order, ctx_id * 2, 2, 0), 2 * BLK)
    yh = lax.axis_index("yh")
    near = jnp.where(yh == 0, placed[:, 0], placed[:, 1])
    far = jnp.where(yh == 0, placed[:, 1], placed[:, 0])
    near = jnp.where(near[:, None] < mine[None, :], 0.0, -1e30).astype(jnp.float32)
    far = jnp.where(far[:, None] < mine[None, :], 0.0, -1e30).astype(jnp.float32)

    scores = 8 * BLK * 2 * n_z * quarter
    cost = pl.CostEstimate(flops=scores * 4 * HD, bytes_accessed=2 << 20, transcendentals=scores)
    sums = jax.ShapeDtypeStruct((n_x, HD + 16, 4 * BLK), jnp.bfloat16)
    for kernel, keys, bias, shape in ((more_kernel, taken, near, state), (last_kernel, other, far, sums)):
        parts = pl.pallas_call(
            kernel,
            out_shape=shape,
            in_specs=[VMEM] * 4,
            out_specs=VMEM,
            compiler_params=params,
            cost_estimate=cost,
            name="attend_more",
        )(queries, keys, bias, parts)
    parts = lax.all_to_all(parts, "x", 0, 0)
    return pl.pallas_call(
        combine_kernel,
        out_shape=jax.ShapeDtypeStruct((tokens, 2 * HD), jnp.bfloat16),
        in_specs=[VMEM],
        out_specs=VMEM,
        name="combine",
    )(parts)


def solution(mesh):
    shape = mesh.shape
    grid = mesh.devices.reshape(2, shape["segment"] // 2, shape["ctx"] // 2, 2, shape["head"])
    fine = Mesh(grid, ("yl", "core", "z", "yh", "x"))
    return jax.shard_map(
        body,
        mesh=fine,
        in_specs=(
            P(SEG, CTX, "x"),
            P(None, "x", SEG),
            P(CTX, (*SEG, "x")),
            P(CTX, SEG),
            P(CTX, SEG),
            P(),
        ),
        out_specs=P(CTX, (*SEG, "x")),
        check_vma=False,
    )
```

```python
import jax
import jax.numpy as jnp
from jax import lax
from jax.experimental import pallas as pl
from jax.experimental.pallas import tpu as pltpu
from jax.sharding import Mesh, PartitionSpec as P

HD = 64
BLK = 128
SEG = ("yl", "core")
CTX = ("z", "yh")
VMEM = pl.BlockSpec(memory_space=pltpu.VMEM)
DIM0 = (((0,), (0,)), ((), ()))


def pack_kernel(query_ref, key_ref, value_ref, out_ref):
    turned = jnp.concatenate([key_ref[...], value_ref[...]], axis=0).astype(jnp.float32)
    chunk = query_ref.shape[0]
    whole = chunk // 16 * 16
    out_ref[whole:] = jnp.zeros((out_ref.shape[0] - whole, out_ref.shape[1]), out_ref.dtype)
    out_ref[:chunk, : query_ref.shape[1]] = query_ref[...]
    out_ref[:chunk, query_ref.shape[1] :] = turned.T.astype(jnp.bfloat16)


def split_kernel(rows_ref, low_ref, high_ref):
    split = low_ref.shape[0]
    low_ref[...] = rows_ref[:split]
    high_ref[...] = rows_ref[split:]


def merge_kernel(low_ref, high_ref, weight_hbm, place_ref, partial_ref, embed_ref, hold_ref, weight_ref, arrived):
    copies = []
    for k in range(3):
        copies.append(pltpu.make_async_copy(weight_hbm.at[k], weight_ref.at[k], arrived.at[k]))
        copies[-1].start()
    split, total = low_ref.shape[1], weight_ref.shape[1]
    chunks, chunk, _ = partial_ref.shape
    hold_ref[:split] = low_ref[3].astype(jnp.float32)
    hold_ref[split:] = high_ref[3].astype(jnp.float32)
    embed_ref[...] = jnp.zeros_like(embed_ref)
    for half in range(2):
        first, second = hold_ref[pl.ds(half * chunk, chunk), :], hold_ref[pl.ds((2 + half) * chunk, chunk), :]
        block = jnp.where(place_ref[0] == 0, first, second).astype(jnp.bfloat16)
        for i in range(chunks):
            embed_ref[2 * i + half, :chunk] = block
    acc = None
    for k in range(3):
        copies[k].wait()
        for ref, rows in ((low_ref, slice(0, split)), (high_ref, slice(split, total))):
            term = lax.dot_general(weight_ref[k, rows, :], ref[k], DIM0, preferred_element_type=jnp.float32)
            acc = term if acc is None else acc + term
    hold_ref[...] = acc
    for i in range(chunks):
        partial_ref[i] = hold_ref[pl.ds(i * chunk, chunk), :]


def settle_kernel(parts_ref, out_ref):
    total = parts_ref[0]
    for i in range(1, parts_ref.shape[0]):
        total = total + parts_ref[i]
    out_ref[...] = jnp.zeros_like(out_ref)
    out_ref[: parts_ref.shape[1]] = total.astype(jnp.bfloat16)


def spread_kernel(block_ref, out_ref):
    count = block_ref.shape[0]
    for i in range(out_ref.shape[0] // count):
        out_ref[i * count : (i + 1) * count] = block_ref[...]


def project_kernel(
    embed_own, embed_other, merged_own, merged_other, weights_hbm, place_ref,
    query_ref, sent_ref, own_ref, rows_ref, weights_ref, arrived,
):
    core, x_id = place_ref[0], place_ref[1]
    copy = pltpu.make_async_copy(weights_hbm, weights_ref, arrived)
    copy.start()
    chunks = embed_own.shape[0]
    _, chunk, tokens = rows_ref.shape
    width = 2 * chunks * chunk
    for kind, pair in enumerate(((embed_own, embed_other), (merged_own, merged_other))):
        total = jnp.zeros((1, tokens), jnp.float32)
        for ref in pair:
            for i in range(chunks):
                part = ref[i, :chunk].astype(jnp.float32)
                total = total + jnp.sum(part * part, axis=0, keepdims=True)
        scale = lax.rsqrt(total / width + 1e-06)
        for ref, side in zip(pair, (core, 1 - core)):
            for i in range(chunks):
                if kind == 0:
                    at = i // 2 * 4 + 2 * side + i % 2
                else:
                    at = 2 * chunks + (2 * (i % 2) + side) * 4 + i // 2
                rows_ref[at] = (ref[i, :chunk].astype(jnp.float32) * scale).astype(jnp.bfloat16)
    acc = jnp.zeros((weights_ref.shape[2], tokens), jnp.float32)
    copy.wait()
    for at in range(weights_ref.shape[0]):
        acc = acc + lax.dot_general(
            weights_ref[at, :chunk], rows_ref[at], DIM0, preferred_element_type=jnp.float32
        )
    half = acc.shape[0] // 2
    query_ref[...] = acc[:half].astype(jnp.bfloat16)
    rows = acc[half:].T.astype(jnp.bfloat16)
    size = own_ref.shape[0]
    quarter = rows[:size]
    for i in range(1, tokens // size):
        quarter = jnp.where(x_id == i, rows[i * size : (i + 1) * size], quarter)
    for i in range(sent_ref.shape[0]):
        sent_ref[i] = quarter
    own_ref[...] = quarter


def heads_of(query_ref, source):
    zeros = jnp.zeros((HD, BLK), jnp.bfloat16)
    pieces = []
    for a in range(2):
        for g in range(2):
            piece = query_ref[source, g * HD : (g + 1) * HD, a * BLK : (a + 1) * BLK]
            pieces.append(jnp.concatenate([piece * jnp.bfloat16(0.125), zeros], axis=0))
    return jnp.concatenate(pieces, axis=1)


def attend_keys(queries, keys_ref, bias_ref, state):
    top, total, accum = state
    groups, chunk, _ = keys_ref.shape
    keys = keys_ref[...].reshape(groups * chunk, 2 * HD)
    bias = bias_ref[...]
    scores = jnp.dot(keys, queries, preferred_element_type=jnp.float32)
    scores = scores.reshape(groups, chunk, queries.shape[1])
    highest = jnp.max(scores, axis=1) + bias
    new_top = jnp.maximum(top, jnp.max(highest, axis=0, keepdims=True))
    weights = jnp.exp(scores + (bias - new_top)[:, None, :])
    rescale = jnp.exp(top - new_top)
    weights = weights.reshape(groups * chunk, queries.shape[1])
    total = total * rescale + jnp.sum(weights, axis=0, keepdims=True)
    mixed = lax.dot_general(keys, weights.astype(jnp.bfloat16), DIM0, preferred_element_type=jnp.float32)
    return new_top, total, accum * rescale + mixed[HD:]


def store_state(out_ref, source, state):
    top, total, accum = state
    out_ref[source, :HD] = accum
    row = lax.broadcasted_iota(jnp.int32, (8, accum.shape[1]), 0)
    out_ref[source, HD:] = jnp.where(row == 0, top, total)


def own_kernel(query_ref, own_ref, place_ref, out_ref):
    x_id = place_ref[1]
    own = own_ref[...]
    chunk = own.shape[0]
    lanes = out_ref.shape[2]
    key_row = lax.broadcasted_iota(jnp.int32, (chunk, lanes), 0) + (x_id % 2) * chunk
    lane = lax.broadcasted_iota(jnp.int32, (chunk, lanes), 1)
    own_bias = jnp.where((lane // (2 * BLK) == x_id // 2) & (key_row <= lane % BLK), 0.0, -1e30)
    for source in range(query_ref.shape[0]):
        queries = heads_of(query_ref, source)
        scores = jnp.dot(own, queries, preferred_element_type=jnp.float32) + own_bias
        top = jnp.maximum(jnp.max(scores, axis=0, keepdims=True), -1e20)
        weights = jnp.exp(scores - top)
        total = jnp.sum(weights, axis=0, keepdims=True)
        accum = lax.dot_general(own, weights.astype(jnp.bfloat16), DIM0, preferred_element_type=jnp.float32)
        store_state(out_ref, source, (top, total, accum[HD:]))


def load_state(state_ref, source):
    rows = (slice(HD, HD + 1), slice(HD + 1, HD + 2), slice(0, HD))
    return tuple(state_ref[source, r, :] for r in rows)


def more_kernel(query_ref, keys_ref, bias_ref, state_ref, out_ref):
    for source in range(query_ref.shape[0]):
        state = load_state(state_ref, source)
        store_state(out_ref, source, attend_keys(heads_of(query_ref, source), keys_ref, bias_ref, state))


def thirds(value):
    high = value.astype(jnp.bfloat16).astype(jnp.float32)
    middle = (value - high).astype(jnp.bfloat16).astype(jnp.float32)
    return high, middle, value - high - middle


def last_kernel(query_ref, keys_ref, bias_ref, state_ref, out_ref):
    for source in range(query_ref.shape[0]):
        top, total, accum = attend_keys(
            heads_of(query_ref, source), keys_ref, bias_ref, load_state(state_ref, source)
        )
        out_ref[source, :HD] = accum.astype(jnp.bfloat16)
        row = lax.broadcasted_iota(jnp.int32, (out_ref.shape[1] - HD, accum.shape[1]), 0)
        rest = jnp.zeros(row.shape, jnp.float32)
        for at, term in enumerate((*thirds(top), *thirds(total))):
            rest = jnp.where(row == at, term, rest)
        out_ref[source, HD:] = rest.astype(jnp.bfloat16)


def combine_kernel(parts_ref, out_ref):
    count = parts_ref.shape[0]
    tops, totals = [], []
    for i in range(count):
        rest = parts_ref[i, HD:, :].astype(jnp.float32)
        tops.append(rest[0:1] + rest[1:2] + rest[2:3])
        totals.append(rest[3:4] + rest[4:5] + rest[5:6])
    top = tops[0]
    for i in range(1, count):
        top = jnp.maximum(top, tops[i])
    total = jnp.zeros_like(top)
    accum = jnp.zeros((HD, parts_ref.shape[2]), jnp.float32)
    for i in range(count):
        share = jnp.exp(tops[i] - top)
        total = total + totals[i] * share
        accum = accum + parts_ref[i, :HD, :].astype(jnp.float32) * share
    result = accum / total
    for a in range(2):
        left = result[:, 2 * a * BLK : (2 * a + 1) * BLK]
        right = result[:, (2 * a + 1) * BLK : (2 * a + 2) * BLK]
        out_ref[a * BLK : (a + 1) * BLK, :] = jnp.concatenate([left, right], axis=0).T.astype(jnp.bfloat16)


def body(hidden, merge_weight, query_weight, key_weight, value_weight, block_order):
    tokens, features = hidden.shape[1:]
    n_x, n_seg = lax.axis_size("x"), lax.axis_size(SEG)
    n_ctx = lax.axis_size(CTX)
    x_id, core, ctx_id = lax.axis_index("x"), lax.axis_index("core"), lax.axis_index(CTX)
    chunk = features // n_seg
    smem, hbm = pl.BlockSpec(memory_space=pltpu.SMEM), pl.BlockSpec(memory_space=pltpu.HBM)
    place = jnp.stack([core, x_id]).astype(jnp.int32)

    padded = (chunk + 7) // 8 * 8
    packed = pl.pallas_call(
        pack_kernel,
        out_shape=jax.ShapeDtypeStruct((padded, 4 * HD), jnp.bfloat16),
        in_specs=[VMEM] * 3,
        out_specs=VMEM,
        name="pack",
    )(query_weight, key_weight.T, value_weight.T)
    weights = lax.all_gather(packed, "yh", axis=0)
    weights = lax.all_gather(weights, "z", axis=0)
    weights = weights.reshape(n_ctx, *weights.shape[2:])

    turned = hidden[0].T
    split = (features // 2 + 15) // 16 * 16
    low, high = pl.pallas_call(
        split_kernel,
        out_shape=tuple(jax.ShapeDtypeStruct((n, tokens), turned.dtype) for n in (split, features - split)),
        in_specs=[VMEM],
        out_specs=(VMEM, VMEM),
        name="split",
    )(turned)
    low = lax.all_gather(low, SEG, axis=0)
    high = lax.all_gather(high, SEG, axis=0)

    partial, embed = pl.pallas_call(
        merge_kernel,
        out_shape=(
            jax.ShapeDtypeStruct((n_x, chunk, tokens), jnp.float32),
            jax.ShapeDtypeStruct((2 * n_x, padded, tokens), jnp.bfloat16),
        ),
        in_specs=[VMEM, VMEM, hbm, smem],
        out_specs=(VMEM, VMEM),
        scratch_shapes=[
            pltpu.VMEM((features, tokens), jnp.float32),
            pltpu.VMEM(merge_weight.shape, merge_weight.dtype),
            pltpu.SemaphoreType.DMA((3,)),
        ],
        compiler_params=pltpu.CompilerParams(vmem_limit_bytes=50 << 20),
        name="merge",
    )(low, high, merge_weight, place)
    parts = lax.all_to_all(partial, "x", 0, 0)
    merged = pl.pallas_call(
        settle_kernel,
        out_shape=jax.ShapeDtypeStruct((padded, tokens), jnp.bfloat16),
        in_specs=[VMEM],
        out_specs=VMEM,
        name="settle",
    )(parts)
    merged = lax.all_gather(merged, "yl", axis=0)
    merged = pl.pallas_call(
        spread_kernel,
        out_shape=jax.ShapeDtypeStruct((2 * n_x, padded, tokens), jnp.bfloat16),
        in_specs=[VMEM],
        out_specs=VMEM,
        name="spread",
    )(merged)

    def over_x(copies):
        own = lax.all_to_all(copies, "x", 0, 0, tiled=True)
        return own, lax.ppermute(own, "core", [(0, 1), (1, 0)])

    embed_own, embed_other = over_x(embed)
    merged_own, merged_other = over_x(merged)

    quarter = tokens // n_x
    params = pltpu.CompilerParams(vmem_limit_bytes=40 << 20)
    n_z, n_yh = lax.axis_size("z"), lax.axis_size("yh")
    query, sent, own = pl.pallas_call(
        project_kernel,
        out_shape=(
            jax.ShapeDtypeStruct((2 * HD, tokens), jnp.bfloat16),
            jax.ShapeDtypeStruct((n_z, quarter, 2 * HD), jnp.bfloat16),
            jax.ShapeDtypeStruct((quarter, 2 * HD), jnp.bfloat16),
        ),
        in_specs=[VMEM] * 4 + [hbm, smem],
        out_specs=(VMEM, VMEM, VMEM),
        scratch_shapes=[
            pltpu.VMEM((n_ctx, chunk, tokens), jnp.bfloat16),
            pltpu.VMEM(weights.shape, weights.dtype),
            pltpu.SemaphoreType.DMA,
        ],
        compiler_params=pltpu.CompilerParams(vmem_limit_bytes=48 << 20),
        name="project",
    )(embed_own, embed_other, merged_own, merged_other, weights, place)
    taken = lax.all_to_all(sent, "z", 0, 0)
    queries = lax.all_gather(query, "x", axis=0)
    state = jax.ShapeDtypeStruct((n_x, HD + 8, 4 * BLK), jnp.float32)
    parts = pl.pallas_call(
        own_kernel,
        out_shape=state,
        in_specs=[VMEM] * 2 + [smem],
        out_specs=VMEM,
        compiler_params=params,
        name="attend_own",
    )(queries, own, place)
    taken, queries, parts = lax.optimization_barrier((taken, queries, parts))
    other = lax.ppermute(taken, "yh", [(0, 1), (1, 0)])

    placed = block_order.reshape(n_z, n_yh, 2)
    placed = jnp.where(x_id < n_x // 2, placed[:, :, 0], placed[:, :, 1])
    mine = jnp.repeat(lax.dynamic_slice_in_dim(block_order, ctx_id * 2, 2, 0), 2 * BLK)
    yh = lax.axis_index("yh")
    near = jnp.where(yh == 0, placed[:, 0], placed[:, 1])
    far = jnp.where(yh == 0, placed[:, 1], placed[:, 0])
    near = jnp.where(near[:, None] < mine[None, :], 0.0, -1e30).astype(jnp.float32)
    far = jnp.where(far[:, None] < mine[None, :], 0.0, -1e30).astype(jnp.float32)

    scores = 8 * BLK * 2 * n_z * quarter
    cost = pl.CostEstimate(flops=scores * 4 * HD, bytes_accessed=2 << 20, transcendentals=scores)
    sums = jax.ShapeDtypeStruct((n_x, HD + 16, 4 * BLK), jnp.bfloat16)
    for kernel, keys, bias, shape in ((more_kernel, taken, near, state), (last_kernel, other, far, sums)):
        parts = pl.pallas_call(
            kernel,
            out_shape=shape,
            in_specs=[VMEM] * 4,
            out_specs=VMEM,
            compiler_params=params,
            cost_estimate=cost,
            name="attend_more",
        )(queries, keys, bias, parts)
    parts = lax.all_to_all(parts, "x", 0, 0)
    return pl.pallas_call(
        combine_kernel,
        out_shape=jax.ShapeDtypeStruct((tokens, 2 * HD), jnp.bfloat16),
        in_specs=[VMEM],
        out_specs=VMEM,
        name="combine",
    )(parts)


def solution(mesh):
    shape = mesh.shape
    grid = mesh.devices.reshape(2, shape["segment"] // 2, shape["ctx"] // 2, 2, shape["head"])
    fine = Mesh(grid, ("yl", "core", "z", "yh", "x"))
    return jax.shard_map(
        body,
        mesh=fine,
        in_specs=(
            P(SEG, CTX, "x"),
            P(None, "x", SEG),
            P(CTX, (*SEG, "x")),
            P(CTX, SEG),
            P(CTX, SEG),
            P(),
        ),
        out_specs=P(CTX, (*SEG, "x")),
        check_vma=False,
    )
```

```python
import jax
import jax.numpy as jnp
from jax import lax
from jax.experimental import pallas as pl
from jax.experimental.pallas import tpu as pltpu
from jax.sharding import Mesh, PartitionSpec as P

HD = 64
BLK = 128
SEG = ("yl", "core")
CTX = ("z", "yh")
VMEM = pl.BlockSpec(memory_space=pltpu.VMEM)
DIM0 = (((0,), (0,)), ((), ()))


def pack_kernel(query_ref, key_ref, value_ref, out_ref):
    turned = jnp.concatenate([key_ref[...], value_ref[...]], axis=0).astype(jnp.float32)
    chunk = query_ref.shape[0]
    whole = chunk // 16 * 16
    out_ref[whole:] = jnp.zeros((out_ref.shape[0] - whole, out_ref.shape[1]), out_ref.dtype)
    out_ref[:chunk, : query_ref.shape[1]] = query_ref[...]
    out_ref[:chunk, query_ref.shape[1] :] = turned.T.astype(jnp.bfloat16)


def split_kernel(rows_ref, low_ref, high_ref):
    split = low_ref.shape[0]
    low_ref[...] = rows_ref[:split]
    high_ref[...] = rows_ref[split:]


def merge_kernel(low_ref, high_ref, weight_hbm, place_ref, partial_ref, embed_ref, hold_ref, weight_ref, arrived):
    copies = []
    for k in range(3):
        copies.append(pltpu.make_async_copy(weight_hbm.at[k], weight_ref.at[k], arrived.at[k]))
        copies[-1].start()
    split, total = low_ref.shape[1], weight_ref.shape[1]
    chunks, chunk, _ = partial_ref.shape
    hold_ref[:split] = low_ref[3].astype(jnp.float32)
    hold_ref[split:] = high_ref[3].astype(jnp.float32)
    embed_ref[...] = jnp.zeros_like(embed_ref)
    for half in range(2):
        first, second = hold_ref[pl.ds(half * chunk, chunk), :], hold_ref[pl.ds((2 + half) * chunk, chunk), :]
        block = jnp.where(place_ref[0] == 0, first, second).astype(jnp.bfloat16)
        for i in range(chunks):
            embed_ref[2 * i + half, :chunk] = block
    acc = None
    for k in range(3):
        copies[k].wait()
        for ref, rows in ((low_ref, slice(0, split)), (high_ref, slice(split, total))):
            term = lax.dot_general(weight_ref[k, rows, :], ref[k], DIM0, preferred_element_type=jnp.float32)
            acc = term if acc is None else acc + term
    hold_ref[...] = acc
    for i in range(chunks):
        partial_ref[i] = hold_ref[pl.ds(i * chunk, chunk), :]


def settle_kernel(parts_ref, out_ref):
    total = parts_ref[0]
    for i in range(1, parts_ref.shape[0]):
        total = total + parts_ref[i]
    out_ref[...] = jnp.zeros_like(out_ref)
    out_ref[: parts_ref.shape[1]] = total.astype(jnp.bfloat16)


def spread_kernel(block_ref, out_ref):
    count = block_ref.shape[0]
    for i in range(out_ref.shape[0] // count):
        out_ref[i * count : (i + 1) * count] = block_ref[...]


def project_kernel(
    embed_own, embed_other, merged_own, merged_other, weights_hbm, place_ref,
    query_ref, sent_ref, own_ref, rows_ref, weights_ref, arrived,
):
    core, x_id = place_ref[0], place_ref[1]
    copy = pltpu.make_async_copy(weights_hbm, weights_ref, arrived)
    copy.start()
    chunks = embed_own.shape[0]
    _, chunk, tokens = rows_ref.shape
    width = 2 * chunks * chunk
    for kind, pair in enumerate(((embed_own, embed_other), (merged_own, merged_other))):
        total = jnp.zeros((1, tokens), jnp.float32)
        for ref in pair:
            for i in range(chunks):
                part = ref[i, :chunk].astype(jnp.float32)
                total = total + jnp.sum(part * part, axis=0, keepdims=True)
        scale = lax.rsqrt(total / width + 1e-06)
        for ref, side in zip(pair, (core, 1 - core)):
            for i in range(chunks):
                if kind == 0:
                    at = i // 2 * 4 + 2 * side + i % 2
                else:
                    at = 2 * chunks + (2 * (i % 2) + side) * 4 + i // 2
                rows_ref[at] = (ref[i, :chunk].astype(jnp.float32) * scale).astype(jnp.bfloat16)
    acc = jnp.zeros((weights_ref.shape[2], tokens), jnp.float32)
    copy.wait()
    for at in range(weights_ref.shape[0]):
        acc = acc + lax.dot_general(
            weights_ref[at, :chunk], rows_ref[at], DIM0, preferred_element_type=jnp.float32
        )
    half = acc.shape[0] // 2
    query_ref[...] = acc[:half].astype(jnp.bfloat16)
    rows = acc[half:].T.astype(jnp.bfloat16)
    size = own_ref.shape[0]
    quarter = rows[:size]
    for i in range(1, tokens // size):
        quarter = jnp.where(x_id == i, rows[i * size : (i + 1) * size], quarter)
    for i in range(sent_ref.shape[0]):
        sent_ref[i] = quarter
    own_ref[...] = quarter


def heads_of(query_ref, source):
    zeros = jnp.zeros((HD, BLK), jnp.bfloat16)
    pieces = []
    for a in range(2):
        for g in range(2):
            piece = query_ref[source, g * HD : (g + 1) * HD, a * BLK : (a + 1) * BLK]
            pieces.append(jnp.concatenate([piece * jnp.bfloat16(0.125), zeros], axis=0))
    return jnp.concatenate(pieces, axis=1)


def attend_keys(queries, keys_ref, bias_ref, state):
    top, total, accum = state
    groups, chunk, _ = keys_ref.shape
    keys = keys_ref[...].reshape(groups * chunk, 2 * HD)
    bias = bias_ref[...]
    scores = jnp.dot(keys, queries, preferred_element_type=jnp.float32)
    scores = scores.reshape(groups, chunk, queries.shape[1])
    highest = jnp.max(scores, axis=1) + bias
    new_top = jnp.maximum(top, jnp.max(highest, axis=0, keepdims=True))
    weights = jnp.exp(scores + (bias - new_top)[:, None, :])
    rescale = jnp.exp(top - new_top)
    weights = weights.reshape(groups * chunk, queries.shape[1])
    total = total * rescale + jnp.sum(weights, axis=0, keepdims=True)
    mixed = lax.dot_general(keys, weights.astype(jnp.bfloat16), DIM0, preferred_element_type=jnp.float32)
    return new_top, total, accum * rescale + mixed[HD:]


def store_state(out_ref, source, state):
    top, total, accum = state
    out_ref[source, :HD] = accum
    row = lax.broadcasted_iota(jnp.int32, (8, accum.shape[1]), 0)
    out_ref[source, HD:] = jnp.where(row == 0, top, total)


def own_kernel(query_ref, own_ref, place_ref, out_ref, ready_ref):
    x_id = place_ref[1]
    own = own_ref[...]
    chunk = own.shape[0]
    lanes = out_ref.shape[2]
    key_row = lax.broadcasted_iota(jnp.int32, (chunk, lanes), 0) + (x_id % 2) * chunk
    lane = lax.broadcasted_iota(jnp.int32, (chunk, lanes), 1)
    own_bias = jnp.where((lane // (2 * BLK) == x_id // 2) & (key_row <= lane % BLK), 0.0, -1e30)
    for source in range(query_ref.shape[0]):
        queries = heads_of(query_ref, source)
        ready_ref[source] = queries
        scores = jnp.dot(own, queries, preferred_element_type=jnp.float32) + own_bias
        top = jnp.maximum(jnp.max(scores, axis=0, keepdims=True), -1e20)
        weights = jnp.exp(scores - top)
        total = jnp.sum(weights, axis=0, keepdims=True)
        accum = lax.dot_general(own, weights.astype(jnp.bfloat16), DIM0, preferred_element_type=jnp.float32)
        store_state(out_ref, source, (top, total, accum[HD:]))


def load_state(state_ref, source):
    rows = (slice(HD, HD + 1), slice(HD + 1, HD + 2), slice(0, HD))
    return tuple(state_ref[source, r, :] for r in rows)


def more_kernel(ready_ref, keys_ref, bias_ref, state_ref, out_ref):
    for source in range(ready_ref.shape[0]):
        state = load_state(state_ref, source)
        store_state(out_ref, source, attend_keys(ready_ref[source], keys_ref, bias_ref, state))


def thirds(value):
    high = value.astype(jnp.bfloat16).astype(jnp.float32)
    middle = (value - high).astype(jnp.bfloat16).astype(jnp.float32)
    return high, middle, value - high - middle


def last_kernel(ready_ref, keys_ref, bias_ref, state_ref, out_ref):
    for source in range(ready_ref.shape[0]):
        state = load_state(state_ref, source)
        top, total, accum = attend_keys(ready_ref[source], keys_ref, bias_ref, state)
        out_ref[source, :HD] = accum.astype(jnp.bfloat16)
        row = lax.broadcasted_iota(jnp.int32, (out_ref.shape[1] - HD, accum.shape[1]), 0)
        rest = jnp.zeros(row.shape, jnp.float32)
        for at, term in enumerate((*thirds(top), *thirds(total))):
            rest = jnp.where(row == at, term, rest)
        out_ref[source, HD:] = rest.astype(jnp.bfloat16)


def combine_kernel(parts_ref, out_ref):
    count = parts_ref.shape[0]
    tops, totals = [], []
    for i in range(count):
        rest = parts_ref[i, HD:, :].astype(jnp.float32)
        tops.append(rest[0:1] + rest[1:2] + rest[2:3])
        totals.append(rest[3:4] + rest[4:5] + rest[5:6])
    top = tops[0]
    for i in range(1, count):
        top = jnp.maximum(top, tops[i])
    total = jnp.zeros_like(top)
    accum = jnp.zeros((HD, parts_ref.shape[2]), jnp.float32)
    for i in range(count):
        share = jnp.exp(tops[i] - top)
        total = total + totals[i] * share
        accum = accum + parts_ref[i, :HD, :].astype(jnp.float32) * share
    result = accum / total
    for a in range(2):
        left = result[:, 2 * a * BLK : (2 * a + 1) * BLK]
        right = result[:, (2 * a + 1) * BLK : (2 * a + 2) * BLK]
        out_ref[a * BLK : (a + 1) * BLK, :] = jnp.concatenate([left, right], axis=0).T.astype(jnp.bfloat16)


def body(hidden, merge_weight, query_weight, key_weight, value_weight, block_order):
    tokens, features = hidden.shape[1:]
    n_x, n_seg = lax.axis_size("x"), lax.axis_size(SEG)
    n_ctx = lax.axis_size(CTX)
    x_id, core, ctx_id = lax.axis_index("x"), lax.axis_index("core"), lax.axis_index(CTX)
    chunk = features // n_seg
    smem, hbm = pl.BlockSpec(memory_space=pltpu.SMEM), pl.BlockSpec(memory_space=pltpu.HBM)
    place = jnp.stack([core, x_id]).astype(jnp.int32)

    padded = (chunk + 7) // 8 * 8
    packed = pl.pallas_call(
        pack_kernel,
        out_shape=jax.ShapeDtypeStruct((padded, 4 * HD), jnp.bfloat16),
        in_specs=[VMEM] * 3,
        out_specs=VMEM,
        name="pack",
    )(query_weight, key_weight.T, value_weight.T)
    weights = lax.all_gather(packed, "yh", axis=0)
    weights = lax.all_gather(weights, "z", axis=0)
    weights = weights.reshape(n_ctx, *weights.shape[2:])

    turned = hidden[0].T
    split = (features // 2 + 15) // 16 * 16
    low, high = pl.pallas_call(
        split_kernel,
        out_shape=tuple(jax.ShapeDtypeStruct((n, tokens), turned.dtype) for n in (split, features - split)),
        in_specs=[VMEM],
        out_specs=(VMEM, VMEM),
        name="split",
    )(turned)
    low = lax.all_gather(low, SEG, axis=0)
    high = lax.all_gather(high, SEG, axis=0)

    partial, embed = pl.pallas_call(
        merge_kernel,
        out_shape=(
            jax.ShapeDtypeStruct((n_x, chunk, tokens), jnp.float32),
            jax.ShapeDtypeStruct((2 * n_x, padded, tokens), jnp.bfloat16),
        ),
        in_specs=[VMEM, VMEM, hbm, smem],
        out_specs=(VMEM, VMEM),
        scratch_shapes=[
            pltpu.VMEM((features, tokens), jnp.float32),
            pltpu.VMEM(merge_weight.shape, merge_weight.dtype),
            pltpu.SemaphoreType.DMA((3,)),
        ],
        compiler_params=pltpu.CompilerParams(vmem_limit_bytes=50 << 20),
        name="merge",
    )(low, high, merge_weight, place)
    parts = lax.all_to_all(partial, "x", 0, 0)
    merged = pl.pallas_call(
        settle_kernel,
        out_shape=jax.ShapeDtypeStruct((padded, tokens), jnp.bfloat16),
        in_specs=[VMEM],
        out_specs=VMEM,
        name="settle",
    )(parts)
    merged = lax.all_gather(merged, "yl", axis=0)
    merged = pl.pallas_call(
        spread_kernel,
        out_shape=jax.ShapeDtypeStruct((2 * n_x, padded, tokens), jnp.bfloat16),
        in_specs=[VMEM],
        out_specs=VMEM,
        name="spread",
    )(merged)

    def over_x(copies):
        own = lax.all_to_all(copies, "x", 0, 0, tiled=True)
        return own, lax.ppermute(own, "core", [(0, 1), (1, 0)])

    embed_own, embed_other = over_x(embed)
    merged_own, merged_other = over_x(merged)

    quarter = tokens // n_x
    params = pltpu.CompilerParams(vmem_limit_bytes=40 << 20)
    n_z, n_yh = lax.axis_size("z"), lax.axis_size("yh")
    query, sent, own = pl.pallas_call(
        project_kernel,
        out_shape=(
            jax.ShapeDtypeStruct((2 * HD, tokens), jnp.bfloat16),
            jax.ShapeDtypeStruct((n_z, quarter, 2 * HD), jnp.bfloat16),
            jax.ShapeDtypeStruct((quarter, 2 * HD), jnp.bfloat16),
        ),
        in_specs=[VMEM] * 4 + [hbm, smem],
        out_specs=(VMEM, VMEM, VMEM),
        scratch_shapes=[
            pltpu.VMEM((n_ctx, chunk, tokens), jnp.bfloat16),
            pltpu.VMEM(weights.shape, weights.dtype),
            pltpu.SemaphoreType.DMA,
        ],
        compiler_params=pltpu.CompilerParams(vmem_limit_bytes=48 << 20),
        name="project",
    )(embed_own, embed_other, merged_own, merged_other, weights, place)
    taken = lax.all_to_all(sent, "z", 0, 0)
    queries = lax.all_gather(query, "x", axis=0)
    state = jax.ShapeDtypeStruct((n_x, HD + 8, 4 * BLK), jnp.float32)
    parts, queries = pl.pallas_call(
        own_kernel,
        out_shape=(state, jax.ShapeDtypeStruct((n_x, 2 * HD, 4 * BLK), jnp.bfloat16)),
        in_specs=[VMEM] * 2 + [smem],
        out_specs=(VMEM, VMEM),
        compiler_params=params,
        name="attend_own",
    )(queries, own, place)
    taken, queries, parts = lax.optimization_barrier((taken, queries, parts))
    other = lax.ppermute(taken, "yh", [(0, 1), (1, 0)])

    placed = block_order.reshape(n_z, n_yh, 2)
    placed = jnp.where(x_id < n_x // 2, placed[:, :, 0], placed[:, :, 1])
    mine = jnp.repeat(lax.dynamic_slice_in_dim(block_order, ctx_id * 2, 2, 0), 2 * BLK)
    yh = lax.axis_index("yh")
    near = jnp.where(yh == 0, placed[:, 0], placed[:, 1])
    far = jnp.where(yh == 0, placed[:, 1], placed[:, 0])
    near = jnp.where(near[:, None] < mine[None, :], 0.0, -1e30).astype(jnp.float32)
    far = jnp.where(far[:, None] < mine[None, :], 0.0, -1e30).astype(jnp.float32)

    scores = 8 * BLK * 2 * n_z * quarter
    cost = pl.CostEstimate(flops=scores * 4 * HD, bytes_accessed=2 << 20, transcendentals=scores)
    sums = jax.ShapeDtypeStruct((n_x, HD + 16, 4 * BLK), jnp.bfloat16)
    for kernel, keys, bias, shape in ((more_kernel, taken, near, state), (last_kernel, other, far, sums)):
        parts = pl.pallas_call(
            kernel,
            out_shape=shape,
            in_specs=[VMEM] * 4,
            out_specs=VMEM,
            compiler_params=params,
            cost_estimate=cost,
            name="attend_more",
        )(queries, keys, bias, parts)
    parts = lax.all_to_all(parts, "x", 0, 0)
    return pl.pallas_call(
        combine_kernel,
        out_shape=jax.ShapeDtypeStruct((tokens, 2 * HD), jnp.bfloat16),
        in_specs=[VMEM],
        out_specs=VMEM,
        name="combine",
    )(parts)


def solution(mesh):
    shape = mesh.shape
    grid = mesh.devices.reshape(2, shape["segment"] // 2, shape["ctx"] // 2, 2, shape["head"])
    fine = Mesh(grid, ("yl", "core", "z", "yh", "x"))
    return jax.shard_map(
        body,
        mesh=fine,
        in_specs=(
            P(SEG, CTX, "x"),
            P(None, "x", SEG),
            P(CTX, (*SEG, "x")),
            P(CTX, SEG),
            P(CTX, SEG),
            P(),
        ),
        out_specs=P(CTX, (*SEG, "x")),
        check_vma=False,
    )
```
